32 devices in a mesh: joined: 4 (over z), view: 8 (over y, x, core).
Axes of the slice: x: 2, y: 2, z: 4, core: 2. Of those that a mesh axis runs over, the one named last changes fastest.
Arguments:
- estimate: float32 [8, 512, 2048], P('view', 'joined'), may hold values from 0.5 to 2
- views: float32 [8, 4, 512, 2048], P('view', None, 'joined'), may hold values from 0.25 to 4
- psf: float32 [4, 2, 65], replicated, may hold values from 0.2 to 2
- offsets: int32 [4, 2], replicated, may hold values from -16 to 16, as said below
- lengths: int32 [4, 2], replicated, may hold values from 1 to 4, as said below
Outputs:
- deconvolved: float32 [8, 512, 2048], P('view', 'joined')
The draws below stay inside these ranges and needn't reach their ends.
Inputs may be any that keep to these rules, and one draw needn't show every extreme that they name: `offsets`: offsets along each lateral dimension reach both -16 and 16 in every draw. `lengths`: in every depth block some view has all 4 planes.
All inputs are finite; a program needn't handle non-finite values.
Results may differ from the reference program's by a relative error of at most 0.0001.
Values sent between devices are 32-bit elements; how exact they have to be, the bound alone decides.
No kernel may reach another device: no remote copies, remote signals or barrier semaphores. Data moves between devices by JAX's collectives and lax.ppermute only.
A program may use at most 128 MiB of HBM per device.

```python
import math
import jax
import jax.numpy as jnp

TAPS = 65
MAXD = 16
RADIUS = 32
BLOCKS = 2
ITERS = 1
NY = 2048
VIEWS = 4
ZB = 4
DEPTH = 8
NX = 512


def draw_offsets(key, part):
    first, second, third = jax.random.split(jax.random.fold_in(key, 11), 3)
    values = jax.random.randint(first, (VIEWS, 2), -MAXD, MAXD + 1)
    upper = jax.random.randint(second, (2,), 0, VIEWS)
    step_on = jax.random.randint(third, (2,), 1, max(VIEWS, 2))
    lower = jnp.mod(upper + step_on, VIEWS)
    members = jnp.arange(VIEWS, dtype=jnp.int32)[:, None]
    values = jnp.where(members == lower[None, :], -MAXD, values)
    values = jnp.where(members == upper[None, :], MAXD, values)
    return values.astype(jnp.int32)


def draw_lengths(key, part):
    first, second = jax.random.split(jax.random.fold_in(key, 23), 2)
    values = jax.random.randint(first, (VIEWS, BLOCKS), 1, ZB + 1)
    full_member = jax.random.randint(second, (BLOCKS,), 0, VIEWS)
    members = jnp.arange(VIEWS, dtype=jnp.int32)[:, None]
    values = jnp.where(members == full_member[None, :], ZB, values)
    return values.astype(jnp.int32)


def shard_levels(key, shape, pieces, least, top_value):
    gain = 1.0
    for dim, blocks in pieces:
        heights = jax.random.uniform(jax.random.fold_in(jax.random.fold_in(key, 6), dim), (blocks,), jnp.float32, least / len(pieces), top_value / len(pieces))
        gain = gain * jnp.repeat(jnp.exp(heights), shape[dim] // blocks).reshape((-1,) + (1,) * (len(shape) - 1 - dim))
    return gain


def setup_inputs(seed: int = 0) -> dict:
    key_of = jax.random.split(jax.random.key(seed), 6)
    return {
        "estimate": jnp.clip(jnp.exp(math.log(2.0) - 1.3862944 * jax.random.uniform(key_of[0], (DEPTH, NX, NY), jnp.float32) ** shard_levels(key_of[0], (DEPTH, NX, NY), ((0, 8), (1, 4)), -0.2, 0.2)), 0.5, 2.0),
        "views": jnp.clip(jnp.exp(math.log(4.0) - 2.7725887 * jax.random.uniform(key_of[1], (VIEWS * BLOCKS, ZB, NX, NY), jnp.float32) ** shard_levels(key_of[1], (VIEWS * BLOCKS, ZB, NX, NY), ((0, 8), (2, 4)), -0.2, 0.2)), 0.25, 4.0),
        "psf": jnp.clip(jnp.exp(jax.random.uniform(key_of[2], (VIEWS, 2, TAPS), jnp.float32, math.log(0.2), math.log(2.0))), 0.2, 2.0),
        "offsets": draw_offsets(jax.random.fold_in(key_of[5], 71), 0),
        "lengths": draw_lengths(jax.random.fold_in(key_of[5], 71), 0),
    }


def line_kernel(taps, shift, length):
    index = jnp.mod(RADIUS - jnp.arange(TAPS, dtype=jnp.int32) - shift, length)
    return jnp.zeros((length,), jnp.float32).at[index].add(taps)


def reference(estimate, views, psf, offsets, lengths):
    stacks = views.reshape(VIEWS, BLOCKS, ZB, NX, NY)
    planes = jnp.arange(ZB, dtype=jnp.int32)
    live = (planes[None, None, :] < lengths[:, :, None]).astype(jnp.float32)
    count = jnp.sum(live, axis=0)
    spectra = []
    for member in range(VIEWS):
        kernel_x = psf[member, 0] / jnp.sum(psf[member, 0])
        kernel_y = psf[member, 1] / jnp.sum(psf[member, 1])
        line_x = line_kernel(kernel_x, offsets[member, 0], NX)
        line_y = line_kernel(kernel_y, offsets[member, 1], NY)
        spectra.append(jnp.fft.rfft2(line_x[:, None] * line_y[None, :]))
    current = estimate.reshape(BLOCKS, ZB, NX, NY)
    for step in range(ITERS):
        transform = jnp.fft.rfft2(current, axes=(-2, -1))
        correction = jnp.zeros_like(current)
        for member in range(VIEWS):
            image = jnp.fft.irfft2(transform * spectra[member], s=(NX, NY), axes=(-2, -1))
            ratio = live[member][:, :, None, None] * stacks[member] / image
            back = jnp.fft.irfft2(jnp.fft.rfft2(ratio, axes=(-2, -1)) * jnp.conj(spectra[member]), s=(NX, NY), axes=(-2, -1))
            correction = correction + back
        current = current * correction / count[:, :, None, None]
    return current.reshape(DEPTH, NX, NY)
```

```python
import functools

import jax
import jax.numpy as jnp
from jax import lax
from jax.experimental import pallas as pl
from jax.experimental.pallas import tpu as pltpu
from jax.sharding import PartitionSpec as P

MAXD = 16
BLOCKS = 2
LANES = 128
F32 = jnp.float32
BF16 = jnp.bfloat16
VMEM_LIMIT = 48 * 1024 * 1024


def split(x):
    hi = x.astype(BF16)
    return hi, (x - hi.astype(F32)).astype(BF16)


def mm(a, b):
    return jnp.dot(a, b, preferred_element_type=F32)


def toeplitz(row, rows, shift, width):
    turned = pltpu.roll(jnp.broadcast_to(row, (8, width)), lax.rem(shift + 4 * width, width), 1)
    wide = jnp.broadcast_to(turned[0:1], (rows, width))
    return pltpu.roll(wide, 0, 1, stride=1, stride_axis=0)


def lateral_factors(row, shift):
    width = row.shape[1]
    left = toeplitz(row, LANES, shift, width)[:, :LANES]
    right = toeplitz(row, LANES, shift + LANES, width)[:, :LANES]
    hi, lo = split(jnp.concatenate([left, right], axis=1))
    return jnp.concatenate([hi, hi], axis=0), lo


def forward_kernel(radius, cut, scal, taps, est, above, below, *rest):
    outs, scratch = rest[:-4], rest[-4:]
    e_hi, e_lo, lhs, _ = scratch
    slot = pl.program_id(0)
    slots = scal.shape[1]
    margin = radius + MAXD
    tile, cols = est.shape
    extended = tile + 2 * margin
    blocks = cols // LANES

    @pl.when(slot == 0)
    def _():
        for piece, at in ((above, 0), (est, margin), (below, margin + tile)):
            rolled = pltpu.roll(piece[...], margin, 1)
            hi, lo = split(rolled)
            e_hi[at : at + piece.shape[0], :] = hi
            e_lo[at : at + piece.shape[0], :] = lo

    dx, dy = scal[0, slot], scal[1, slot]
    live = scal[2, slot].astype(F32)
    width = taps.shape[2]
    gx, gyr = taps[0, 0:1, :], taps[0, 3:4, :]
    band = toeplitz(gx, tile, dx + MAXD, width)[:, :extended]
    b_hi, b_lo = split(band)
    both = mm(jnp.concatenate([b_hi, b_lo], axis=0), e_hi[...])
    blurred = both[:tile] + both[tile:] + mm(b_hi, e_lo[...])
    hi, lo = split(blurred)
    for j in range(blocks):
        at = slice(j * LANES, (j + 1) * LANES)
        lhs[j * tile : (j + 1) * tile, :LANES] = hi[:, at]
        lhs[j * tile : (j + 1) * tile, LANES:] = lo[:, at]
    first, second = lateral_factors(gyr, -dy - MAXD - 2 * radius)
    part = mm(lhs[...], first) + mm(lhs[:, :LANES], second)
    for j in range(blocks):
        n = (j + 1) % blocks
        image = part[j * tile : (j + 1) * tile, :LANES] + part[n * tile : (n + 1) * tile, LANES:]
        value = live / image
        for out, (c0, c1) in zip(outs[:-1], cut):
            if c0 <= j < c1:
                at = slice((j - c0) * LANES, (j - c0 + 1) * LANES)
                out[0, :margin, at] = value[:margin]
                out[0, margin:, at] = value[tile - margin :]
        outs[-1][0, :, j * LANES : (j + 1) * LANES] = value[margin : tile - margin]


def ratio_blurred(slot, value, lhs, taps, dy, radius):
    rows, cols = value.shape
    hi, lo = split(value)
    blocks = cols // LANES
    for j in range(blocks):
        at = slice(j * LANES, (j + 1) * LANES)
        lhs[j * rows : (j + 1) * rows, :LANES] = hi[:, at]
        lhs[j * rows : (j + 1) * rows, LANES:] = lo[:, at]
    first, second = lateral_factors(taps[slot, 2:3, :], dy + MAXD - LANES)
    part = mm(lhs[...], first) + mm(lhs[:, :LANES], second)
    return [part[j * rows : (j + 1) * rows] for j in range(blocks)]


def slot_values(slot, half, kept, sib):
    return kept[slot][0] if slot < half else sib[slot - half]


def edge_kernel(radius, tile, is_first, is_last, half, scal, taps, rim, sib, *rest):
    kept, rest = rest[:half], rest[half:]
    if not is_first:
        (carry_left, *rest) = rest
    if is_last and not is_first:
        (carry_right, *rest) = rest
    main, up, down = rest[:3]
    rest = rest[3:]
    if not is_last:
        (next_left, *rest) = rest
    if is_first and not is_last:
        (next_right, *rest) = rest
    lhs, s_hi, s_lo = rest
    slots = 2 * half
    margin = radius + MAXD
    extended = tile + 2 * margin
    width = taps.shape[2]
    bands = []
    for slot in range(slots):
        dx, dy = scal[0, slot], scal[1, slot]
        value = slot_values(slot, half, kept, sib) * rim[slot]
        parts = ratio_blurred(slot, value, lhs, taps, dy, radius)
        lefts = [x[:, :LANES] for x in parts]
        rights = [x[:, LANES:] for x in parts]
        if not is_first:
            lefts = [carry_left[slot]] + lefts
        else:
            if is_last:
                closing = rights[0]
            else:
                next_right[slot] = rights[0]
            rights = rights[1:]
        if is_last:
            rights = rights + [closing if is_first else carry_right[slot]]
        else:
            next_left[slot] = lefts[-1]
            lefts = lefts[:-1]
        base = slot * tile
        for j, (left, right) in enumerate(zip(lefts, rights)):
            at = slice(j * LANES, (j + 1) * LANES)
            hi, lo = split(left + right)
            for ref, piece in ((s_hi, hi), (s_lo, lo)):
                ref[base : base + margin, at] = piece[:margin]
                ref[base + margin : base + tile - margin, at] = jnp.zeros((tile - 2 * margin, LANES), BF16)
                ref[base + tile - margin : base + tile, at] = piece[margin:]
        gxr = taps[slot, 1:2, :]
        bands.append(toeplitz(gxr, extended, -dx - MAXD - 2 * radius, width)[:, :tile])
    b_hi, b_lo = split(jnp.concatenate(bands, axis=1))
    both = mm(jnp.concatenate([b_hi, b_lo], axis=0), s_hi[...])
    total = both[:extended] + both[extended:] + mm(b_hi, s_lo[...])
    up[...] = total[:margin]
    main[...] = total[margin : margin + tile]
    down[...] = total[margin + tile :]


def final_kernel(radius, tile, half, nchunks, scal, inv, taps, rim, sib, est, *rest):
    kept, rest = rest[:half], rest[half:]
    chunks, rest = rest[: 3 * nchunks], rest[3 * nchunks :]
    out, lhs, s_hi, s_lo, total = rest
    slots = 2 * half
    margin = radius + MAXD
    mid = tile - 2 * margin
    cols = est.shape[1]
    blocks = cols // LANES
    wide = 2 * LANES * max(1, slots * mid // LANES)
    lane = lax.broadcasted_iota(jnp.int32, (tile, wide), 1)
    band = jnp.zeros((tile, wide), F32)
    for slot in range(slots):
        dx, dy = scal[0, slot], scal[1, slot]
        value = slot_values(slot, half, kept, sib) * rim[slot]
        parts = ratio_blurred(slot, value, lhs, taps, dy, radius)
        base = slot * mid
        for j in range(1, blocks + 1):
            at = slice((j - 1) * LANES, j * LANES)
            hi, lo = split(parts[j - 1][:, :LANES] + parts[j % blocks][:, LANES:])
            s_hi[base : base + mid, at] = hi
            s_lo[base : base + mid, at] = lo
        gxr = taps[slot, 1:2, :]
        if wide > gxr.shape[1]:
            gxr = jnp.concatenate([gxr, jnp.zeros((1, wide - gxr.shape[1]), F32)], axis=1)
        line = toeplitz(gxr, tile, base - dx - MAXD - 2 * radius, wide)
        band = jnp.where((lane >= base) & (lane < base + mid), line, band)
    b_hi, b_lo = split(band[:, : slots * mid])
    both = mm(jnp.concatenate([b_hi, b_lo], axis=0), s_hi[...])
    total[...] = both[:tile] + both[tile:] + mm(b_hi, s_lo[...])
    at = 0
    for c in range(nchunks):
        main, above, below = chunks[3 * c : 3 * c + 3]
        w = main.shape[1]
        total[:, at : at + w] += main[...]
        total[:margin, at : at + w] += above[...]
        total[tile - margin :, at : at + w] += below[...]
        at += w
    turned = pltpu.roll(total[...], LANES - margin, 1)
    out[...] = est[...] * turned * inv[0]


def whole_spec(shape):
    return pl.BlockSpec(shape, lambda i, *_: (0,) * len(shape))


def params():
    return pltpu.CompilerParams(vmem_limit_bytes=VMEM_LIMIT, dimension_semantics=("arbitrary",))


def forward(radius, cut, scal, taps, est, above, below):
    slots = taps.shape[0]
    tile, cols = est.shape
    margin = radius + MAXD
    widths = [(c1 - c0) * LANES for c0, c1 in cut]
    shapes = [(slots, 2 * margin, w) for w in widths] + [(slots, tile - 2 * margin, cols)]
    extended = tile + 2 * margin
    return pl.pallas_call(
        functools.partial(forward_kernel, radius, cut),
        grid_spec=pltpu.PrefetchScalarGridSpec(
            num_scalar_prefetch=1,
            grid=(slots,),
            in_specs=[
                pl.BlockSpec((1,) + taps.shape[1:], lambda i, *_: (i, 0, 0)),
                whole_spec(est.shape),
                whole_spec(above.shape),
                whole_spec(below.shape),
            ],
            out_specs=[pl.BlockSpec((1,) + s[1:], lambda i, *_: (i, 0, 0)) for s in shapes],
            scratch_shapes=[
                pltpu.VMEM((extended, cols), BF16),
                pltpu.VMEM((extended, cols), BF16),
                pltpu.VMEM((tile * cols // LANES, 2 * LANES), BF16),
                pltpu.SMEM((1,), jnp.int32),
            ],
        ),
        out_shape=[jax.ShapeDtypeStruct(s, F32) for s in shapes],
        compiler_params=params(),
        name="forward",
    )(scal, taps, est, above, below)


def kept_spec(array):
    shape = (1,) + array.shape[1:]
    return pl.BlockSpec(shape, lambda i, scal, *_: (scal[3, 0], 0, 0))


def edges(radius, tile, is_first, is_last, scal, taps, rim, sib, kept, carries):
    half = len(kept)
    slots = 2 * half
    margin = radius + MAXD
    blocks = rim.shape[2] // LANES
    made = (blocks - (1 if is_first else 0) + (1 if is_last else 0)) * LANES
    shapes = [(tile, made), (margin, made), (margin, made)]
    carried = (slots, 2 * margin, LANES)
    if not is_last:
        shapes.append(carried)
        if is_first:
            shapes.append(carried)
    operands = [taps, rim, sib]
    return pl.pallas_call(
        functools.partial(edge_kernel, radius, tile, is_first, is_last, half),
        grid_spec=pltpu.PrefetchScalarGridSpec(
            num_scalar_prefetch=1,
            grid=(1,),
            in_specs=[whole_spec(x.shape) for x in operands]
            + [kept_spec(x) for x in kept]
            + [whole_spec(x.shape) for x in carries],
            out_specs=[whole_spec(s) for s in shapes],
            scratch_shapes=[
                pltpu.VMEM((blocks * 2 * margin, 2 * LANES), BF16),
                pltpu.VMEM((slots * tile, made), BF16),
                pltpu.VMEM((slots * tile, made), BF16),
            ],
        ),
        out_shape=[jax.ShapeDtypeStruct(s, F32) for s in shapes],
        compiler_params=params(),
        name="edges",
    )(scal, *operands, *kept, *carries)


def finish(radius, scal, inv, taps, rim, sib, est, kept, chunks):
    half = len(kept)
    slots = 2 * half
    margin = radius + MAXD
    tile, cols = est.shape
    mid = tile - 2 * margin
    operands = [taps, rim, sib, est]
    flat = [x for chunk in chunks for x in chunk]
    return pl.pallas_call(
        functools.partial(final_kernel, radius, tile, half, len(chunks)),
        grid_spec=pltpu.PrefetchScalarGridSpec(
            num_scalar_prefetch=2,
            grid=(1,),
            in_specs=[whole_spec(x.shape) for x in operands]
            + [kept_spec(x) for x in kept]
            + [whole_spec(x.shape) for x in flat],
            out_specs=whole_spec(est.shape),
            scratch_shapes=[
                pltpu.VMEM((cols // LANES * mid, 2 * LANES), BF16),
                pltpu.VMEM((slots * mid, cols), BF16),
                pltpu.VMEM((slots * mid, cols), BF16),
                pltpu.VMEM((tile, cols), F32),
            ],
        ),
        out_shape=jax.ShapeDtypeStruct(est.shape, F32),
        compiler_params=params(),
        name="finish",
    )(scal, inv, *operands, *kept, *flat)


def per_device(estimate, views, psf, offsets, lengths):
    size = lax.axis_size("view")
    joined = lax.axis_size("joined")
    position = lax.axis_index("view")
    members = size // BLOCKS
    half = members // 2
    member, block = position // BLOCKS, position % BLOCKS
    planes, tile, cols = views.shape[1:]
    radius = (psf.shape[2] - 1) // 2
    margin = radius + MAXD
    stack = views[0]
    est = estimate[0]
    total_blocks = cols // LANES

    up = [(i, (i + 1) % joined) for i in range(joined)]
    down = [(j, i) for i, j in up]
    above = lax.ppermute(est[tile - margin :], "joined", up)
    below = lax.ppermute(est[:margin], "joined", down)

    pair, core = position // 2, position % 2
    owned_block, place = pair // half, pair % half
    row = position % planes

    def slot_view(c, s):
        return c * half + (place - s - (c == owned_block).astype(jnp.int32)) % half

    order = [slot_view(core, s) for s in range(half)] + [slot_view(1 - core, s) for s in range(half)]
    order = jnp.stack(order).astype(jnp.int32)
    weights = psf / jnp.sum(psf, axis=2, keepdims=True)
    taps = jnp.stack(
        [weights[:, 0], weights[:, 0, ::-1], weights[:, 1], weights[:, 1, ::-1]], axis=1
    )
    taps = jnp.pad(taps, ((0, 0), (0, 0), (0, 2 * LANES - taps.shape[2])))
    taps = taps[order]
    shifts = offsets[order]
    reach = lax.dynamic_index_in_dim(lengths, owned_block, 1, keepdims=False)
    live = (row < reach).astype(jnp.int32)
    inv = (1.0 / jnp.sum(live).astype(F32)).reshape(1)
    scal = jnp.stack(
        [shifts[:, 0], shifts[:, 1], live[order], jnp.full((members,), core, jnp.int32)]
    ).astype(jnp.int32)

    def target(p, s):
        k, b = p // BLOCKS, p % BLOCKS
        t = (k % half + s + (1 if k // half == b else 0)) % half
        return 2 * (b * half + t) + k // half

    def exchange(cut_rows):
        kept = []
        for s in range(half):
            t = (member % half + s + (member // half == block).astype(jnp.int32)) % half
            payload = cut_rows(lax.dynamic_slice_in_dim(stack, 2 * t, 2, 0))
            kept.append(lax.ppermute(payload, "view", [(p, target(p, s)) for p in range(size)]))
        other = jnp.concatenate(
            [lax.dynamic_slice_in_dim(x, 1 - core, 1, 0) for x in kept], axis=0
        )
        return kept, lax.ppermute(other, "view", [(p, p ^ 1) for p in range(size)])

    first = total_blocks * 5 // 8
    cut = ((0, first), (first, total_blocks))

    def edge_rows(c0, c1):
        def take(x):
            x = x[:, :, c0 * LANES : c1 * LANES]
            return jnp.concatenate([x[:, :margin], x[:, tile - margin :]], axis=1)

        return take

    received = [exchange(edge_rows(c0, c1)) for c0, c1 in cut]
    middle = exchange(lambda x: x[:, margin : tile - margin])

    rims = forward(radius, cut, scal, taps, est, above, below)

    chunks, carries, closing = [], [], None
    for i, (kept, sib) in enumerate(received):
        is_first, is_last = i == 0, i == len(cut) - 1
        given = [] if is_first else [carries] + ([closing] if is_last else [])
        result = edges(radius, tile, is_first, is_last, scal, taps, rims[i], sib, kept, given)
        main, upper, lower = result[:3]
        if not is_last:
            carries = result[3]
            if is_first:
                closing = result[4]
        from_above = lax.ppermute(lower, "joined", up)
        from_below = lax.ppermute(upper, "joined", down)
        chunks.append((main, from_above, from_below))
    kept, sib = middle
    out = finish(radius, scal, inv, taps, rims[-1], sib, est, kept, chunks)
    return out[None]


def solution(mesh):
    return jax.shard_map(
        per_device,
        mesh=mesh,
        in_specs=(P("view", "joined", None), P("view", None, "joined", None), P(), P(), P()),
        out_specs=P("view", "joined", None),
        check_vma=False,
    )
```

```python
import functools

import jax
import jax.numpy as jnp
from jax import lax
from jax.experimental import pallas as pl
from jax.experimental.pallas import tpu as pltpu
from jax.sharding import PartitionSpec as P

MAXD = 16
BLOCKS = 2
LANES = 128
F32 = jnp.float32
BF16 = jnp.bfloat16
VMEM_LIMIT = 28 * 1024 * 1024


def split(x):
    hi = x.astype(BF16)
    return hi, (x - hi.astype(F32)).astype(BF16)


def mm(a, b):
    return jnp.dot(a, b, preferred_element_type=F32)


def toeplitz(row, rows, shift, width):
    turned = pltpu.roll(jnp.broadcast_to(row, (8, width)), lax.rem(shift + 4 * width, width), 1)
    wide = jnp.broadcast_to(turned[0:1], (rows, width))
    return pltpu.roll(wide, 0, 1, stride=1, stride_axis=0)


def lateral_factors(row, shift):
    width = row.shape[1]
    left = toeplitz(row, LANES, shift, width)[:, :LANES]
    right = toeplitz(row, LANES, shift + LANES, width)[:, :LANES]
    hi, lo = split(jnp.concatenate([left, right], axis=1))
    return jnp.concatenate([hi, hi], axis=0), lo


def fetch(source, target, sem):
    copy = pltpu.make_async_copy(source, target, sem)
    copy.start()
    return copy


def forward_kernel(radius, cut, scal, taps, est, above, below, *rest):
    outs, (e_hi, e_lo, lhs, halo, sems) = rest[:-5], rest[-5:]
    slot = pl.program_id(0)
    margin = radius + MAXD
    tile, cols = est.shape
    extended = tile + 2 * margin
    blocks = cols // LANES

    @pl.when(slot == 0)
    def _():
        copies = [fetch(x, halo.at[i], sems.at[i]) for i, x in enumerate((above, below))]
        for piece, at, copy in (
            (est, margin, None),
            (halo.at[0], 0, copies[0]),
            (halo.at[1], margin + tile, copies[1]),
        ):
            if copy is not None:
                copy.wait()
            top, rest = split(pltpu.roll(piece[...], margin, 1))
            e_hi[at : at + piece.shape[0], :] = top
            e_lo[at : at + piece.shape[0], :] = rest

    dx, dy = scal[0, slot], scal[1, slot]
    live = scal[2, slot].astype(F32)
    width = taps.shape[2]
    gx, gyr = taps[0, 0:1, :], taps[0, 3:4, :]
    band = toeplitz(gx, tile, dx + MAXD, width)[:, :extended]
    b_hi, b_lo = split(band)
    both = mm(jnp.concatenate([b_hi, b_lo], axis=0), e_hi[...])
    blurred = both[:tile] + both[tile:] + mm(b_hi, e_lo[...])
    hi, lo = split(blurred)
    for j in range(blocks):
        at = slice(j * LANES, (j + 1) * LANES)
        lhs[j * tile : (j + 1) * tile, :LANES] = hi[:, at]
        lhs[j * tile : (j + 1) * tile, LANES:] = lo[:, at]
    first, second = lateral_factors(gyr, -dy - MAXD - 2 * radius)
    part = mm(lhs[...], first) + mm(lhs[:, :LANES], second)
    for j in range(blocks):
        n = (j + 1) % blocks
        image = part[j * tile : (j + 1) * tile, :LANES] + part[n * tile : (n + 1) * tile, LANES:]
        value = live / image
        for out, (c0, c1) in zip(outs[:-1], cut):
            if c0 <= j < c1:
                at = slice((j - c0) * LANES, (j - c0 + 1) * LANES)
                out[slot, :margin, at] = value[:margin]
                out[slot, margin:, at] = value[tile - margin :]
        outs[-1][slot, :, j * LANES : (j + 1) * LANES] = value[margin : tile - margin]


def ratio_blurred(slot, value, lhs, taps, dy, radius):
    rows, cols = value.shape
    hi, lo = split(value)
    blocks = cols // LANES
    for j in range(blocks):
        at = slice(j * LANES, (j + 1) * LANES)
        lhs[j * rows : (j + 1) * rows, :LANES] = hi[:, at]
        lhs[j * rows : (j + 1) * rows, LANES:] = lo[:, at]
    first, second = lateral_factors(taps[slot, 2:3, :], dy + MAXD - LANES)
    part = mm(lhs[...], first) + mm(lhs[:, :LANES], second)
    return [part[j * rows : (j + 1) * rows] for j in range(blocks)]


def runs_of(arrays, half, blocks):
    total = half * blocks
    marks = [round(total * i / arrays) for i in range(arrays + 1)]
    result = []
    for lo, hi in zip(marks, marks[1:]):
        runs = []
        for view in range(half):
            c0, c1 = max(lo, view * blocks), min(hi, (view + 1) * blocks)
            if c0 < c1:
                runs.append((view, c0 - view * blocks, c1 - view * blocks))
        result.append(runs)
    return result


def slot_values(slot, half, runs, mine, sib):
    if slot < half:
        return mine[slot][...]
    parts = []
    for ref, of_ref in zip(sib, runs):
        at = 0
        for view, c0, c1 in of_ref:
            width = (c1 - c0) * LANES
            if view == slot - half:
                parts.append(ref[:, at : at + width])
            at += width
    return parts[0] if len(parts) == 1 else jnp.concatenate(parts, axis=1)


def pair_kernel(half, runs, scal, *refs):
    kept, own, refs = refs[:half], refs[half], refs[half + 1 :]
    (buffer, sem), refs = refs[-2:], refs[:-2]
    outs = refs[-(half + len(runs)) :]
    away, inner = scal[half], scal[half + 1]

    @pl.when(inner != 0)
    def _():
        copy = fetch(own, buffer, sem.at[0])
        copy.wait()

    @pl.when(inner == 0)
    def _():
        buffer[...] = kept[half - 1][...]

    sources = [*kept[: half - 1], buffer]
    for s in range(half):
        outs[s][...] = sources[s][1 - away]
    for out, of_out in zip(outs[half:], runs):
        at = 0
        for view, c0, c1 in of_out:
            width = (c1 - c0) * LANES
            out[:, at : at + width] = sources[view][away, :, c0 * LANES : c1 * LANES]
            at += width


def edge_kernel(radius, tile, is_first, is_last, half, runs, scal, taps, rim, *rest):
    mine, sib, rest = rest[:half], rest[half : half + len(runs)], rest[half + len(runs) :]
    carries = []
    if not is_first:
        carries, rest = rest[: 1 + is_last], rest[1 + is_last :]
    main, up, down = rest[:3]
    rest = rest[3:]
    if not is_last:
        (next_left, *rest) = rest
    if is_first and not is_last:
        (next_right, *rest) = rest
    lhs, s_hi, s_lo = rest
    slots = 2 * half
    margin = radius + MAXD
    extended = tile + 2 * margin
    width = taps.shape[2]
    bands = []
    for slot in range(slots):
        dx, dy = scal[0, slot], scal[1, slot]
        value = slot_values(slot, half, runs, mine, sib) * rim[slot]
        parts = ratio_blurred(slot, value, lhs, taps, dy, radius)
        lefts = [x[:, :LANES] for x in parts]
        rights = [x[:, LANES:] for x in parts]
        if not is_first:
            lefts = [carries[0][slot]] + lefts
        else:
            if is_last:
                closing = rights[0]
            else:
                next_right[slot] = rights[0]
            rights = rights[1:]
        if is_last:
            rights = rights + [closing if is_first else carries[1][slot]]
        else:
            next_left[slot] = lefts[-1]
            lefts = lefts[:-1]
        base = slot * tile
        for j, (left, right) in enumerate(zip(lefts, rights)):
            at = slice(j * LANES, (j + 1) * LANES)
            hi, lo = split(left + right)
            for ref, piece in ((s_hi, hi), (s_lo, lo)):
                ref[base : base + margin, at] = piece[:margin]
                ref[base + margin : base + tile - margin, at] = jnp.zeros((tile - 2 * margin, LANES), BF16)
                ref[base + tile - margin : base + tile, at] = piece[margin:]
        gxr = taps[slot, 1:2, :]
        bands.append(toeplitz(gxr, extended, -dx - MAXD - 2 * radius, width)[:, :tile])
    b_hi, b_lo = split(jnp.concatenate(bands, axis=1))
    both = mm(jnp.concatenate([b_hi, b_lo], axis=0), s_hi[...])
    total = both[:extended] + both[extended:] + mm(b_hi, s_lo[...])
    up[...] = total[:margin]
    main[...] = total[margin : margin + tile]
    down[...] = total[margin + tile :]


def final_kernel(radius, tile, half, runs, nchunks, scal, inv, taps, rim, est, *rest):
    mine, sib, rest = rest[:half], rest[half : half + len(runs)], rest[half + len(runs) :]
    chunks, rest = rest[: 3 * nchunks], rest[3 * nchunks :]
    out, lhs, s_hi, s_lo, total, rbuf, field, part, edge, sems = rest
    first = fetch(rim, rbuf, sems.at[0])
    late = [fetch(est, field, sems.at[1])]
    at = 0
    for c in range(nchunks):
        main, above, below = chunks[3 * c : 3 * c + 3]
        w = main.shape[1]
        late.append(fetch(main, part.at[:, at : at + w], sems.at[2 + 3 * c]))
        late.append(fetch(above, edge.at[0, :, at : at + w], sems.at[3 + 3 * c]))
        late.append(fetch(below, edge.at[1, :, at : at + w], sems.at[4 + 3 * c]))
        at += w
    first.wait()
    slots = 2 * half
    margin = radius + MAXD
    mid = tile - 2 * margin
    cols = est.shape[1]
    blocks = cols // LANES
    wide = 2 * LANES * max(1, slots * mid // LANES)
    lane = lax.broadcasted_iota(jnp.int32, (tile, wide), 1)
    band = jnp.zeros((tile, wide), F32)
    for slot in range(slots):
        dx, dy = scal[0, slot], scal[1, slot]
        value = slot_values(slot, half, runs, mine, sib) * rbuf[slot]
        parts = ratio_blurred(slot, value, lhs, taps, dy, radius)
        base = slot * mid
        for j in range(1, blocks + 1):
            at = slice((j - 1) * LANES, j * LANES)
            hi, lo = split(parts[j - 1][:, :LANES] + parts[j % blocks][:, LANES:])
            s_hi[base : base + mid, at] = hi
            s_lo[base : base + mid, at] = lo
        gxr = taps[slot, 1:2, :]
        if wide > gxr.shape[1]:
            gxr = jnp.concatenate([gxr, jnp.zeros((1, wide - gxr.shape[1]), F32)], axis=1)
        line = toeplitz(gxr, tile, base - dx - MAXD - 2 * radius, wide)
        band = jnp.where((lane >= base) & (lane < base + mid), line, band)
    b_hi, b_lo = split(band[:, : slots * mid])
    both = mm(jnp.concatenate([b_hi, b_lo], axis=0), s_hi[...])
    for copy in late:
        copy.wait()
    total[...] = both[:tile] + both[tile:] + mm(b_hi, s_lo[...]) + part[...]
    total[:margin, :] += edge[0]
    total[tile - margin :, :] += edge[1]
    turned = pltpu.roll(total[...], LANES - margin, 1)
    out[...] = field[...] * turned * inv[0]


def light():
    return pl.CostEstimate(flops=0, bytes_accessed=1024, transcendentals=0)


def pack_kernel(starts, pieces, n_in, *refs):
    scal, refs = refs[0], refs[1:]
    ins, outs, sem = refs[:n_in], refs[n_in:-1], refs[-1]
    copies = []
    for i, (src, dst, start, src_at, dst_at) in enumerate(pieces):
        ref = ins[src] if start is None else ins[src].at[pl.ds(scal[start], starts[start])]
        copies.append(fetch(ref.at[src_at], outs[dst].at[dst_at], sem.at[i]))
    for copy in copies:
        copy.wait()


def in_vmem():
    return pl.BlockSpec(memory_space=pltpu.VMEM)


def in_hbm():
    return pl.BlockSpec(memory_space=pltpu.HBM)


def anywhere():
    return pl.BlockSpec(memory_space=pl.ANY)


def from_vmem(operands):
    return [pltpu.with_memory_space_constraint(x, pltpu.VMEM) for x in operands]


def from_hbm(operands):
    return [pltpu.with_memory_space_constraint(x, pltpu.HBM) for x in operands]


def pack(scal, starts, ins, after, shapes, pieces, name):
    return pl.pallas_call(
        functools.partial(pack_kernel, starts, pieces, len(ins) + len(after)),
        grid_spec=pltpu.PrefetchScalarGridSpec(
            num_scalar_prefetch=1,
            grid=(1,),
            in_specs=[in_hbm()] * len(ins) + [anywhere()] * len(after),
            out_specs=[in_vmem()] * len(shapes),
            scratch_shapes=[pltpu.SemaphoreType.DMA((len(pieces),))],
        ),
        out_shape=[jax.ShapeDtypeStruct(s, F32) for s in shapes],
        compiler_params=params(),
        cost_estimate=light(),
        name=name,
    )(scal, *from_hbm(ins), *after)


def part_pair(scal, runs, kept, own, after):
    half = len(kept)
    rows, cols = own.shape[1:]
    shapes = [(rows, cols)] * half
    shapes += [(rows, sum(c1 - c0 for _, c0, c1 in of) * LANES) for of in runs]
    out = pl.pallas_call(
        functools.partial(pair_kernel, half, runs),
        grid_spec=pltpu.PrefetchScalarGridSpec(
            num_scalar_prefetch=1,
            grid=(1,),
            in_specs=[in_vmem()] * half + [in_hbm()] + [anywhere()] * len(after),
            out_specs=[in_vmem()] * len(shapes),
            scratch_shapes=[pltpu.VMEM(own.shape, F32), pltpu.SemaphoreType.DMA((1,))],
        ),
        out_shape=[jax.ShapeDtypeStruct(s, F32) for s in shapes],
        compiler_params=params(),
        cost_estimate=light(),
        name="pair",
    )(scal, *from_vmem(kept), *from_hbm([own]), *after)
    return out[:half], out[half:]


def whole_spec(shape):
    return pl.BlockSpec(shape, lambda i, *_: (0,) * len(shape))


def params():
    return pltpu.CompilerParams(vmem_limit_bytes=VMEM_LIMIT, dimension_semantics=("arbitrary",))


def forward(radius, cut, scal, taps, est, above, below):
    slots = taps.shape[0]
    tile, cols = est.shape
    margin = radius + MAXD
    widths = [(c1 - c0) * LANES for c0, c1 in cut]
    shapes = [(slots, 2 * margin, w) for w in widths] + [(slots, tile - 2 * margin, cols)]
    extended = tile + 2 * margin
    return pl.pallas_call(
        functools.partial(forward_kernel, radius, cut),
        grid_spec=pltpu.PrefetchScalarGridSpec(
            num_scalar_prefetch=1,
            grid=(slots,),
            in_specs=[pl.BlockSpec((1,) + taps.shape[1:], lambda i, *_: (i, 0, 0))]
            + [in_vmem(), in_hbm(), in_hbm()],
            out_specs=[in_vmem()] * len(shapes),
            scratch_shapes=[
                pltpu.VMEM((extended, cols), BF16),
                pltpu.VMEM((extended, cols), BF16),
                pltpu.VMEM((tile * cols // LANES, 2 * LANES), BF16),
                pltpu.VMEM((2, margin, cols), F32),
                pltpu.SemaphoreType.DMA((2,)),
            ],
        ),
        out_shape=[jax.ShapeDtypeStruct(s, F32) for s in shapes],
        compiler_params=params(),
        cost_estimate=light(),
        name="forward",
    )(scal, taps, *from_vmem([est]), *from_hbm([above, below]))


def edges(radius, tile, is_first, is_last, runs, scal, taps, rim, mine, sib, carries):
    half = len(mine)
    slots = 2 * half
    margin = radius + MAXD
    blocks = rim.shape[2] // LANES
    made = (blocks - (1 if is_first else 0) + (1 if is_last else 0)) * LANES
    shapes = [(tile, made), (margin, made), (margin, made)]
    carried = (slots, 2 * margin, LANES)
    if not is_last:
        shapes.append(carried)
        if is_first:
            shapes.append(carried)
    operands = [rim, *mine, *sib, *carries]
    return pl.pallas_call(
        functools.partial(edge_kernel, radius, tile, is_first, is_last, half, runs),
        grid_spec=pltpu.PrefetchScalarGridSpec(
            num_scalar_prefetch=1,
            grid=(1,),
            in_specs=[whole_spec(taps.shape)] + [in_vmem()] * len(operands),
            out_specs=[in_vmem()] * len(shapes),
            scratch_shapes=[
                pltpu.VMEM((blocks * 2 * margin, 2 * LANES), BF16),
                pltpu.VMEM((slots * tile, made), BF16),
                pltpu.VMEM((slots * tile, made), BF16),
            ],
        ),
        out_shape=[jax.ShapeDtypeStruct(s, F32) for s in shapes],
        compiler_params=params(),
        cost_estimate=light(),
        name="edges",
    )(scal, taps, *from_vmem(operands))


def finish(radius, runs, scal, inv, taps, rim, est, mine, sib, chunks):
    half = len(mine)
    slots = 2 * half
    margin = radius + MAXD
    tile, cols = est.shape
    mid = tile - 2 * margin
    flat = [x for chunk in chunks for x in chunk]
    return pl.pallas_call(
        functools.partial(final_kernel, radius, tile, half, runs, len(chunks)),
        grid_spec=pltpu.PrefetchScalarGridSpec(
            num_scalar_prefetch=2,
            grid=(1,),
            in_specs=[whole_spec(taps.shape), in_hbm(), in_hbm()]
            + [in_vmem()] * (half + len(runs))
            + [in_hbm()] * len(flat),
            out_specs=whole_spec(est.shape),
            scratch_shapes=[
                pltpu.VMEM((cols // LANES * mid, 2 * LANES), BF16),
                pltpu.VMEM((slots * mid, cols), BF16),
                pltpu.VMEM((slots * mid, cols), BF16),
                pltpu.VMEM((tile, cols), F32),
                pltpu.VMEM(rim.shape, F32),
                pltpu.VMEM((tile, cols), F32),
                pltpu.VMEM((tile, cols), F32),
                pltpu.VMEM((2, margin, cols), F32),
                pltpu.SemaphoreType.DMA((2 + len(flat),)),
            ],
        ),
        out_shape=jax.ShapeDtypeStruct(est.shape, F32),
        compiler_params=params(),
        cost_estimate=light(),
        name="finish",
    )(scal, inv, taps, *from_hbm([rim, est]), *from_vmem([*mine, *sib]), *from_hbm(flat))


def per_device(estimate, views, psf, offsets, lengths):
    size = lax.axis_size("view")
    joined = lax.axis_size("joined")
    position = lax.axis_index("view")
    members = size // BLOCKS
    half = members // 2
    member, block = position // BLOCKS, position % BLOCKS
    planes, tile, cols = views.shape[1:]
    radius = (psf.shape[2] - 1) // 2
    margin = radius + MAXD
    stack = views[0]
    est = estimate[0]
    total_blocks = cols // LANES

    up = [(i, (i + 1) % joined) for i in range(joined)]
    down = [(j, i) for i, j in up]

    def target(p, s):
        k, b = p // BLOCKS, p % BLOCKS
        t = (k % half + s + (1 if k // half == b else 0)) % half
        return 2 * (b * half + t) + k // half

    first = total_blocks // 2
    cut = ((0, first), (first, total_blocks))
    away = [
        2 * ((member % half + s + (member // half == block).astype(jnp.int32)) % half)
        for s in range(half)
    ]
    inner = (member // half == block).astype(jnp.int32)
    away = jnp.stack(away + [1 - position % 2, inner]).astype(jnp.int32)
    starts = (2,) * half + (1,)
    top, bottom = slice(0, margin), slice(tile - margin, tile)
    low, high = slice(0, margin), slice(margin, 2 * margin)
    every = slice(None)

    def edge_pieces(c0, c1):
        at = slice(c0 * LANES, c1 * LANES)
        pieces = []
        for s in range(half):
            pieces.append((0, s, s, (every, top, at), (every, low)))
            pieces.append((0, s, s, (every, bottom, at), (every, high)))
        return pieces

    def view_send(parts):
        sent = []
        for s, x in enumerate(parts):
            pairs = [(p, target(p, s)) for p in range(size)]
            sent.append(lax.ppermute(x, "view", [(p, q) for p, q in pairs if p != q]))
        return sent

    def pair_send(runs, kept, own, after):
        mine, others = part_pair(away, runs, kept, own, after)
        return mine, [lax.ppermute(x, "view", [(p, p ^ 1) for p in range(size)]) for x in others]

    def edge_shape(c0, c1):
        return (2, 2 * margin, (c1 - c0) * LANES)

    packed_a = pack(
        away, starts, [stack], [], [edge_shape(*cut[0])] * half, edge_pieces(*cut[0]), "pack_first"
    )
    kept_a = view_send(packed_a)
    slab = pack(
        away, starts, [est, psf], packed_a[:1], [(margin, cols)] * 2 + [psf.shape],
        [
            (0, 0, None, (bottom,), (every,)),
            (0, 1, None, (top,), (every,)),
            (1, 2, None, (every,), (every,)),
        ],
        "pack_slab",
    )
    above = lax.ppermute(slab[0], "joined", up)
    below = lax.ppermute(slab[1], "joined", down)
    psf = slab[2]
    packed_b = pack(
        away, starts, [stack], slab[:1], [edge_shape(*cut[1])] * half, edge_pieces(*cut[1]),
        "pack_second",
    )
    kept_b = view_send(packed_b)

    pair, core = position // 2, position % 2
    owned_block, place = pair // half, pair % half
    row = position % planes

    def slot_view(c, s):
        return c * half + (place - s - (c == owned_block).astype(jnp.int32)) % half

    order = [slot_view(core, s) for s in range(half)] + [slot_view(1 - core, s) for s in range(half)]
    order = jnp.stack(order).astype(jnp.int32)
    weights = psf / jnp.sum(psf, axis=2, keepdims=True)
    taps = jnp.stack(
        [weights[:, 0], weights[:, 0, ::-1], weights[:, 1], weights[:, 1, ::-1]], axis=1
    )
    taps = jnp.pad(taps, ((0, 0), (0, 0), (0, 2 * LANES - taps.shape[2])))
    taps = taps[order]
    shifts = offsets[order]
    reach = lax.dynamic_index_in_dim(lengths, owned_block, 1, keepdims=False)
    live = (row < reach).astype(jnp.int32)
    inv = (1.0 / jnp.sum(live).astype(F32)).reshape(1)
    scal = jnp.stack(
        [shifts[:, 0], shifts[:, 1], live[order], jnp.where(jnp.arange(members) == 0, core, (core == owned_block).astype(jnp.int32))]
    ).astype(jnp.int32)

    rims = forward(radius, cut, scal, taps, est, above, below)
    mid = slice(margin, tile - margin)
    packed_c = pack(
        away, starts, [stack], packed_b[:1], [(2, tile - 2 * margin, cols)] * half,
        [(0, s, s, (every, slice(margin, tile - margin)), (every,)) for s in range(half)],
        "pack_third",
    )
    kept_c = view_send(packed_c)

    chunks, carries, main = [], [], None
    for i, (kept, packed) in enumerate(((kept_a, packed_a), (kept_b, packed_b))):
        runs = runs_of(half, half, cut[i][1] - cut[i][0])
        mine, sib = pair_send(runs, kept, packed[-1], rims[-1:] if i == 0 else [main])
        is_first, is_last = i == 0, i == len(cut) - 1
        result = edges(
            radius, tile, is_first, is_last, runs, scal, taps, rims[i], mine, sib, carries
        )
        main, upper, lower = result[:3]
        carries = result[3:]
        from_above = lax.ppermute(lower, "joined", up)
        from_below = lax.ppermute(upper, "joined", down)
        chunks.append((main, from_above, from_below))
    runs = runs_of(3, half, total_blocks)
    mine, sib = pair_send(runs, kept_c, packed_c[-1], [main, *chunks[0][1:]])
    out = finish(radius, runs, scal, inv, taps, rims[-1], est, mine, sib, chunks)
    return out[None]


def solution(mesh):
    return jax.shard_map(
        per_device,
        mesh=mesh,
        in_specs=(P("view", "joined", None), P("view", None, "joined", None), P(), P(), P()),
        out_specs=P("view", "joined", None),
        check_vma=False,
    )
```

```python
import functools

import jax
import jax.numpy as jnp
from jax import lax
from jax.experimental import pallas as pl
from jax.experimental.pallas import tpu as pltpu
from jax.sharding import PartitionSpec as P

MAXD = 16
BLOCKS = 2
LANES = 128
F32 = jnp.float32
BF16 = jnp.bfloat16
VMEM_LIMIT = 28 * 1024 * 1024


def split(x):
    hi = x.astype(BF16)
    return hi, (x - hi.astype(F32)).astype(BF16)


def mm(a, b):
    return jnp.dot(a, b, preferred_element_type=F32)


def toeplitz(row, rows, shift, width):
    turned = pltpu.roll(jnp.broadcast_to(row, (8, width)), lax.rem(shift + 4 * width, width), 1)
    wide = jnp.broadcast_to(turned[0:1], (rows, width))
    return pltpu.roll(wide, 0, 1, stride=1, stride_axis=0)


def lateral_factors(row, shift):
    width = row.shape[1]
    left = toeplitz(row, LANES, shift, width)[:, :LANES]
    right = toeplitz(row, LANES, shift + LANES, width)[:, :LANES]
    hi, lo = split(jnp.concatenate([left, right], axis=1))
    return jnp.concatenate([hi, hi], axis=0), lo


def fetch(source, target, sem):
    copy = pltpu.make_async_copy(source, target, sem)
    copy.start()
    return copy


def fetch_sides(odd, inside, across, target, first_sem, second_sem):
    return [
        fetch(inside, target.at[1 - odd], first_sem),
        fetch(across, target.at[odd], second_sem),
    ]


def forward_kernel(radius, cut, scal, taps, est, inside, across, *rest):
    outs, (e_hi, e_lo, lhs, halo, sems) = rest[:-5], rest[-5:]
    slot = pl.program_id(0)
    margin = radius + MAXD
    tile, cols = est.shape
    extended = tile + 2 * margin
    blocks = cols // LANES

    @pl.when(slot == 0)
    def _():
        copies = fetch_sides(scal[3, 2], inside, across, halo, sems.at[0], sems.at[1])
        for piece, at in ((est, margin), (halo.at[0], 0), (halo.at[1], margin + tile)):
            if at == 0:
                for copy in copies:
                    copy.wait()
            top, rest = split(pltpu.roll(piece[...], margin, 1))
            e_hi[at : at + piece.shape[0], :] = top
            e_lo[at : at + piece.shape[0], :] = rest

    dx, dy = scal[0, slot], scal[1, slot]
    live = scal[2, slot].astype(F32)
    width = taps.shape[2]
    gx, gyr = taps[0, 0:1, :], taps[0, 3:4, :]
    band = toeplitz(gx, tile, dx + MAXD, width)[:, :extended]
    b_hi, b_lo = split(band)
    both = mm(jnp.concatenate([b_hi, b_lo], axis=0), e_hi[...])
    blurred = both[:tile] + both[tile:] + mm(b_hi, e_lo[...])
    hi, lo = split(blurred)
    for j in range(blocks):
        at = slice(j * LANES, (j + 1) * LANES)
        lhs[j * tile : (j + 1) * tile, :LANES] = hi[:, at]
        lhs[j * tile : (j + 1) * tile, LANES:] = lo[:, at]
    first, second = lateral_factors(gyr, -dy - MAXD - 2 * radius)
    part = mm(lhs[...], first) + mm(lhs[:, :LANES], second)
    for j in range(blocks):
        n = (j + 1) % blocks
        image = part[j * tile : (j + 1) * tile, :LANES] + part[n * tile : (n + 1) * tile, LANES:]
        value = live / image
        for out, (c0, c1) in zip(outs[:-1], cut):
            if c0 <= j < c1:
                at = slice((j - c0) * LANES, (j - c0 + 1) * LANES)
                out[slot, :margin, at] = value[:margin]
                out[slot, margin:, at] = value[tile - margin :]
        outs[-1][slot, :, j * LANES : (j + 1) * LANES] = value[margin : tile - margin]


def ratio_blurred(slot, value, lhs, taps, dy, radius):
    rows, cols = value.shape
    hi, lo = split(value)
    blocks = cols // LANES
    for j in range(blocks):
        at = slice(j * LANES, (j + 1) * LANES)
        lhs[j * rows : (j + 1) * rows, :LANES] = hi[:, at]
        lhs[j * rows : (j + 1) * rows, LANES:] = lo[:, at]
    first, second = lateral_factors(taps[slot, 2:3, :], dy + MAXD - LANES)
    part = mm(lhs[...], first) + mm(lhs[:, :LANES], second)
    return [part[j * rows : (j + 1) * rows] for j in range(blocks)]


def runs_of(arrays, half, blocks):
    total = half * blocks
    marks = [round(total * i / arrays) for i in range(arrays + 1)]
    result = []
    for lo, hi in zip(marks, marks[1:]):
        runs = []
        for view in range(half):
            c0, c1 = max(lo, view * blocks), min(hi, (view + 1) * blocks)
            if c0 < c1:
                runs.append((view, c0 - view * blocks, c1 - view * blocks))
        result.append(runs)
    return result


def slot_values(slot, half, runs, mine, sib):
    if slot < half:
        return mine[slot][...]
    parts = []
    for ref, of_ref in zip(sib, runs):
        at = 0
        for view, c0, c1 in of_ref:
            width = (c1 - c0) * LANES
            if view == slot - half:
                parts.append(ref[:, at : at + width])
            at += width
    return parts[0] if len(parts) == 1 else jnp.concatenate(parts, axis=1)


def fetch_either(flag, source, other, target, sem):
    @pl.when(flag != 0)
    def _():
        fetch(other, target, sem)

    @pl.when(flag == 0)
    def _():
        fetch(source, target, sem)

    return pltpu.make_async_copy(source, target, sem)


def pair_kernel(half, runs, scal, *refs):
    kept, own, refs = refs[:half], refs[half], refs[half + 1 :]
    outs, sem = refs[-1 - len(runs) - half : -1], refs[-1]
    away, inner = scal[half], scal[half + 1]
    copies = []
    for out, of_out in zip(outs, runs):
        at = 0
        for view, c0, c1 in of_out:
            cols = slice(c0 * LANES, c1 * LANES)
            target = out.at[:, at : at + (c1 - c0) * LANES]
            place = (kept[view].at[away, :, cols], target, sem.at[len(copies)])
            if view < half - 1:
                copies.append(fetch(*place))
            else:
                copies.append(fetch_either(inner, place[0], own.at[away, :, cols], *place[1:]))
            at += (c1 - c0) * LANES
    for s, out in enumerate(outs[len(runs) :]):
        place = (kept[s].at[1 - away], out, sem.at[len(copies)])
        if s < half - 1:
            copies.append(fetch(*place))
        else:
            copies.append(fetch_either(inner, place[0], own.at[1 - away], *place[1:]))
    for copy in copies:
        copy.wait()


def edge_kernel(radius, tile, is_first, is_last, half, runs, scal, taps, rim, *rest):
    mine, rest = rest[:half], rest[half:]
    sib, rest = rest[: len(runs)], rest[len(runs) :]
    carries = []
    if not is_first:
        carries, rest = rest[: 1 + is_last], rest[1 + is_last :]
    main, inside, across = rest[:3]
    rest = rest[3:]
    if not is_last:
        (next_left, *rest) = rest
    if is_first and not is_last:
        (next_right, *rest) = rest
    lhs, s_hi, s_lo = rest
    slots = 2 * half
    margin = radius + MAXD
    extended = tile + 2 * margin
    width = taps.shape[2]
    bands = []
    for slot in range(slots):
        dx, dy = scal[0, slot], scal[1, slot]
        value = slot_values(slot, half, runs, mine, sib) * rim[slot]
        parts = ratio_blurred(slot, value, lhs, taps, dy, radius)
        lefts = [x[:, :LANES] for x in parts]
        rights = [x[:, LANES:] for x in parts]
        if not is_first:
            lefts = [carries[0][slot]] + lefts
        else:
            if is_last:
                closing = rights[0]
            else:
                next_right[slot] = rights[0]
            rights = rights[1:]
        if is_last:
            rights = rights + [closing if is_first else carries[1][slot]]
        else:
            next_left[slot] = lefts[-1]
            lefts = lefts[:-1]
        base = slot * tile
        for j, (left, right) in enumerate(zip(lefts, rights)):
            at = slice(j * LANES, (j + 1) * LANES)
            hi, lo = split(left + right)
            for ref, piece in ((s_hi, hi), (s_lo, lo)):
                ref[base : base + margin, at] = piece[:margin]
                ref[base + margin : base + tile - margin, at] = jnp.zeros((tile - 2 * margin, LANES), BF16)
                ref[base + tile - margin : base + tile, at] = piece[margin:]
        gxr = taps[slot, 1:2, :]
        bands.append(toeplitz(gxr, extended, -dx - MAXD - 2 * radius, width)[:, :tile])
    b_hi, b_lo = split(jnp.concatenate(bands, axis=1))
    both = mm(jnp.concatenate([b_hi, b_lo], axis=0), s_hi[...])
    total = both[:extended] + both[extended:] + mm(b_hi, s_lo[...])
    odd = scal[3, 2] != 0
    main[...] = total[margin : margin + tile]
    inside[...] = jnp.where(odd, total[:margin], total[margin + tile :])
    across[...] = jnp.where(odd, total[margin + tile :], total[:margin])


def middle_kernel(radius, tile, half, runs, scal, taps, rim, *rest):
    mine, rest = rest[:half], rest[half:]
    sib, rest = rest[: len(runs)], rest[len(runs) :]
    first, second, inside, across, total, lhs, s_hi, s_lo, part, edge, sems = rest
    width = first.shape[1]
    late = [
        fetch(first, part.at[:, :width], sems.at[0]),
        fetch(second, part.at[:, width:], sems.at[1]),
        *fetch_sides(scal[3, 2], inside, across, edge, sems.at[2], sems.at[3]),
    ]
    slots = 2 * half
    margin = radius + MAXD
    mid = tile - 2 * margin
    cols = total.shape[1]
    blocks = cols // LANES
    wide = 2 * LANES * max(1, slots * mid // LANES)
    lane = lax.broadcasted_iota(jnp.int32, (tile, wide), 1)
    band = jnp.zeros((tile, wide), F32)
    for slot in range(slots):
        dx, dy = scal[0, slot], scal[1, slot]
        value = slot_values(slot, half, runs, mine, sib) * rim[slot]
        parts = ratio_blurred(slot, value, lhs, taps, dy, radius)
        base = slot * mid
        for j in range(1, blocks + 1):
            at = slice((j - 1) * LANES, j * LANES)
            hi, lo = split(parts[j - 1][:, :LANES] + parts[j % blocks][:, LANES:])
            s_hi[base : base + mid, at] = hi
            s_lo[base : base + mid, at] = lo
        gxr = taps[slot, 1:2, :]
        if wide > gxr.shape[1]:
            gxr = jnp.concatenate([gxr, jnp.zeros((1, wide - gxr.shape[1]), F32)], axis=1)
        line = toeplitz(gxr, tile, base - dx - MAXD - 2 * radius, wide)
        band = jnp.where((lane >= base) & (lane < base + mid), line, band)
    b_hi, b_lo = split(band[:, : slots * mid])
    both = mm(jnp.concatenate([b_hi, b_lo], axis=0), s_hi[...])
    for copy in late:
        copy.wait()
    total[...] = both[:tile] + both[tile:] + mm(b_hi, s_lo[...]) + part[...]
    total[:margin, :width] += edge[0]
    total[tile - margin :, :width] += edge[1]


def update_kernel(radius, tile, slots, scal, total, est, inside, across, out, edge, sems):
    margin = radius + MAXD
    copies = fetch_sides(scal[3, 2], inside, across, edge, sems.at[0], sems.at[1])
    count = scal[2, 0]
    for slot in range(1, slots):
        count += scal[2, slot]
    width, cols = inside.shape[1], est.shape[1]
    weight = 1.0 / jnp.full((1, cols), count.astype(F32), F32)
    for copy in copies:
        copy.wait()
    at = slice(cols - width, cols)
    total[:margin, at] += edge[0]
    total[tile - margin :, at] += edge[1]
    out[...] = est[...] * weight * pltpu.roll(total[...], LANES - margin, 1)


def light():
    return pl.CostEstimate(flops=0, bytes_accessed=1024, transcendentals=0)


def pack_kernel(starts, pieces, n_in, *refs):
    scal, refs = refs[0], refs[1:]
    ins, outs, sem = refs[:n_in], refs[n_in:-1], refs[-1]
    copies = []
    for i, (src, dst, start, src_at, dst_at) in enumerate(pieces):
        ref = ins[src]
        if start is not None and start < len(starts):
            ref = ref.at[pl.ds(scal[start], starts[start])]
        elif start is not None:
            ref = ref.at[pl.ds(pl.multiple_of(scal[start], 8), outs[dst].shape[0])]
        copies.append(fetch(ref.at[src_at], outs[dst].at[dst_at], sem.at[i]))
    for copy in copies:
        copy.wait()


def in_vmem():
    return pl.BlockSpec(memory_space=pltpu.VMEM)


def in_hbm():
    return pl.BlockSpec(memory_space=pltpu.HBM)


def anywhere():
    return pl.BlockSpec(memory_space=pl.ANY)


def from_vmem(operands):
    return [pltpu.with_memory_space_constraint(x, pltpu.VMEM) for x in operands]


def from_hbm(operands):
    return [pltpu.with_memory_space_constraint(x, pltpu.HBM) for x in operands]


def pack(scal, starts, ins, after, shapes, pieces, name):
    return pl.pallas_call(
        functools.partial(pack_kernel, starts, pieces, len(ins) + len(after)),
        grid_spec=pltpu.PrefetchScalarGridSpec(
            num_scalar_prefetch=1,
            grid=(1,),
            in_specs=[in_hbm()] * len(ins) + [anywhere()] * len(after),
            out_specs=[in_vmem()] * len(shapes),
            scratch_shapes=[pltpu.SemaphoreType.DMA((len(pieces),))],
        ),
        out_shape=[jax.ShapeDtypeStruct(s, F32) for s in shapes],
        compiler_params=params(),
        cost_estimate=light(),
        name=name,
    )(scal, *from_hbm(ins), *after)


def part_pair(scal, runs, kept, own, after):
    half = len(kept)
    rows = own.shape[1]
    shapes = [(rows, sum(c1 - c0 for _, c0, c1 in of) * LANES) for of in runs]
    shapes += [(rows, own.shape[2])] * half
    out = pl.pallas_call(
        functools.partial(pair_kernel, half, runs),
        grid_spec=pltpu.PrefetchScalarGridSpec(
            num_scalar_prefetch=1,
            grid=(1,),
            in_specs=[in_hbm()] * (half + 1) + [anywhere()] * len(after),
            out_specs=[in_vmem()] * len(shapes),
            scratch_shapes=[pltpu.SemaphoreType.DMA((half + sum(len(of) for of in runs),))],
        ),
        out_shape=[jax.ShapeDtypeStruct(s, F32) for s in shapes],
        compiler_params=params(),
        cost_estimate=light(),
        name="pair",
    )(scal, *from_hbm([*kept, own]), *after)
    return out[: len(runs)], out[len(runs) :]


def whole_spec(shape):
    return pl.BlockSpec(shape, lambda i, *_: (0,) * len(shape))


def params():
    return pltpu.CompilerParams(vmem_limit_bytes=VMEM_LIMIT, dimension_semantics=("arbitrary",))


def forward(radius, cut, scal, taps, est, inside, across):
    slots = taps.shape[0]
    tile, cols = est.shape
    margin = radius + MAXD
    widths = [(c1 - c0) * LANES for c0, c1 in cut]
    shapes = [(slots, 2 * margin, w) for w in widths] + [(slots, tile - 2 * margin, cols)]
    extended = tile + 2 * margin
    return pl.pallas_call(
        functools.partial(forward_kernel, radius, cut),
        grid_spec=pltpu.PrefetchScalarGridSpec(
            num_scalar_prefetch=1,
            grid=(slots,),
            in_specs=[pl.BlockSpec((1,) + taps.shape[1:], lambda i, *_: (i, 0, 0))]
            + [in_vmem(), in_hbm(), in_hbm()],
            out_specs=[in_vmem()] * len(shapes),
            scratch_shapes=[
                pltpu.VMEM((extended, cols), BF16),
                pltpu.VMEM((extended, cols), BF16),
                pltpu.VMEM((tile * cols // LANES, 2 * LANES), BF16),
                pltpu.VMEM((2, margin, cols), F32),
                pltpu.SemaphoreType.DMA((2,)),
            ],
        ),
        out_shape=[jax.ShapeDtypeStruct(s, F32) for s in shapes],
        compiler_params=params(),
        cost_estimate=light(),
        name="forward",
    )(scal, taps, *from_vmem([est]), *from_hbm([inside, across]))


def edges(radius, tile, is_first, is_last, runs, scal, taps, rim, mine, sib, carries):
    half = len(mine)
    slots = 2 * half
    margin = radius + MAXD
    blocks = rim.shape[2] // LANES
    made = (blocks - (1 if is_first else 0) + (1 if is_last else 0)) * LANES
    shapes = [(tile, made), (margin, made), (margin, made)]
    carried = (slots, 2 * margin, LANES)
    if not is_last:
        shapes.append(carried)
        if is_first:
            shapes.append(carried)
    return pl.pallas_call(
        functools.partial(edge_kernel, radius, tile, is_first, is_last, half, runs),
        grid_spec=pltpu.PrefetchScalarGridSpec(
            num_scalar_prefetch=1,
            grid=(1,),
            in_specs=[whole_spec(taps.shape)]
            + [in_vmem()] * (1 + half + len(sib) + len(carries)),
            out_specs=[in_vmem()] * len(shapes),
            scratch_shapes=[
                pltpu.VMEM((blocks * 2 * margin, 2 * LANES), BF16),
                pltpu.VMEM((slots * tile, made), BF16),
                pltpu.VMEM((slots * tile, made), BF16),
            ],
        ),
        out_shape=[jax.ShapeDtypeStruct(s, F32) for s in shapes],
        compiler_params=params(),
        cost_estimate=light(),
        name="edges",
    )(scal, taps, *from_vmem([rim, *mine, *sib, *carries]))


def middle(radius, tile, runs, scal, taps, rim, mine, sib, mains, inside, across):
    half = len(mine)
    slots, mid, cols = rim.shape
    margin = radius + MAXD
    return pl.pallas_call(
        functools.partial(middle_kernel, radius, tile, half, runs),
        grid_spec=pltpu.PrefetchScalarGridSpec(
            num_scalar_prefetch=1,
            grid=(1,),
            in_specs=[whole_spec(taps.shape)]
            + [in_vmem()] * (1 + half + len(runs))
            + [anywhere()] * 4,
            out_specs=in_vmem(),
            scratch_shapes=[
                pltpu.VMEM((cols // LANES * mid, 2 * LANES), BF16),
                pltpu.VMEM((slots * mid, cols), BF16),
                pltpu.VMEM((slots * mid, cols), BF16),
                pltpu.VMEM((tile, cols), F32),
                pltpu.VMEM((2,) + inside.shape, F32),
                pltpu.SemaphoreType.DMA((4,)),
            ],
        ),
        out_shape=jax.ShapeDtypeStruct((tile, cols), F32),
        compiler_params=params(),
        cost_estimate=light(),
        name="middle",
    )(scal, taps, *from_vmem([rim, *mine, *sib]), *mains, inside, across)


def update(radius, slots, scal, total, est, inside, across):
    tile = est.shape[0]
    return pl.pallas_call(
        functools.partial(update_kernel, radius, tile, slots),
        grid_spec=pltpu.PrefetchScalarGridSpec(
            num_scalar_prefetch=1,
            grid=(1,),
            in_specs=[in_vmem()] * 2 + [anywhere()] * 2,
            out_specs=whole_spec(est.shape),
            scratch_shapes=[
                pltpu.VMEM((2,) + inside.shape, F32),
                pltpu.SemaphoreType.DMA((2,)),
            ],
        ),
        out_shape=jax.ShapeDtypeStruct(est.shape, F32),
        compiler_params=params(),
        cost_estimate=light(),
        name="update",
    )(scal, *from_vmem([total, est]), inside, across)


def per_device(estimate, views, psf, offsets, lengths):
    size = lax.axis_size("view")
    joined = lax.axis_size("joined")
    position = lax.axis_index("view")
    members = size // BLOCKS
    half = members // 2
    member, block = position // BLOCKS, position % BLOCKS
    planes, tile, cols = views.shape[1:]
    radius = (psf.shape[2] - 1) // 2
    margin = radius + MAXD
    stack = views[0]
    est = estimate[0]
    total_blocks = cols // LANES

    odd = lax.axis_index("joined") % 2
    twin = [(i, i ^ 1) for i in range(joined)]
    other = [(i, (i - 1 if i % 2 == 0 else i + 1) % joined) for i in range(joined)]

    def target(p, s):
        k, b = p // BLOCKS, p % BLOCKS
        t = (k % half + s + (1 if k // half == b else 0)) % half
        return 2 * (b * half + t) + k // half

    first = total_blocks // 2
    cut = ((0, first), (first, total_blocks))
    away = [
        2 * ((member % half + s + (member // half == block).astype(jnp.int32)) % half)
        for s in range(half)
    ]
    inner = (member // half == block).astype(jnp.int32)
    edge_at = (1 - odd) * (tile - margin)
    away = away + [1 - position % 2, inner, edge_at, tile - margin - edge_at]
    away = jnp.stack(away).astype(jnp.int32)
    starts = (2,) * half + (1,)
    top, bottom = slice(0, margin), slice(tile - margin, tile)
    low, high = slice(0, margin), slice(margin, 2 * margin)
    every = slice(None)

    def edge_pieces(c0, c1):
        at = slice(c0 * LANES, c1 * LANES)
        pieces = []
        for s in range(half):
            pieces.append((0, s, s, (every, top, at), (every, low)))
            pieces.append((0, s, s, (every, bottom, at), (every, high)))
        return pieces

    def view_send(parts):
        sent = []
        for s, x in enumerate(parts):
            pairs = [(p, target(p, s)) for p in range(size)]
            sent.append(lax.ppermute(x, "view", [(p, q) for p, q in pairs if p != q]))
        return sent

    def pair_send(runs, kept, own, after):
        others, mine = part_pair(away, runs, kept, own, after)
        return mine, [lax.ppermute(x, "view", [(p, p ^ 1) for p in range(size)]) for x in others]

    def edge_shape(c0, c1):
        return (2, 2 * margin, (c1 - c0) * LANES)

    packed_a = pack(
        away, starts, [stack], [], [edge_shape(*cut[0])] * half, edge_pieces(*cut[0]), "pack_first"
    )
    slab = pack(
        away, starts, [est, psf], packed_a[:1], [(margin, cols)] * 2 + [psf.shape],
        [
            (0, 0, half + 2, (every,), (every,)),
            (0, 1, half + 3, (every,), (every,)),
            (1, 2, None, (every,), (every,)),
        ],
        "pack_slab",
    )
    inside = lax.ppermute(slab[0], "joined", twin)
    across = lax.ppermute(slab[1], "joined", other)
    psf = slab[2]
    kept_a = view_send(packed_a)
    center = slice(margin, tile - margin)
    packed = pack(
        away, starts, [stack], slab[:1],
        [edge_shape(*cut[1])] * half + [(2, tile - 2 * margin, cols)] * half,
        edge_pieces(*cut[1])
        + [(0, half + s, s, (every, center), (every,)) for s in range(half)],
        "pack_second",
    )
    packed_b, packed_c = packed[:half], packed[half:]
    kept_b = view_send(packed_b)
    kept_c = view_send(packed_c)

    pair, core = position // 2, position % 2
    owned_block, place = pair // half, pair % half
    row = position % planes

    def slot_view(c, s):
        return c * half + (place - s - (c == owned_block).astype(jnp.int32)) % half

    order = [slot_view(core, s) for s in range(half)] + [slot_view(1 - core, s) for s in range(half)]
    order = jnp.stack(order).astype(jnp.int32)
    weights = psf / jnp.sum(psf, axis=2, keepdims=True)
    taps = jnp.stack(
        [weights[:, 0], weights[:, 0, ::-1], weights[:, 1], weights[:, 1, ::-1]], axis=1
    )
    taps = jnp.pad(taps, ((0, 0), (0, 0), (0, 2 * LANES - taps.shape[2])))
    taps = taps[order]
    shifts = offsets[order]
    reach = lax.dynamic_index_in_dim(lengths, owned_block, 1, keepdims=False)
    live = (row < reach).astype(jnp.int32)
    side = jnp.stack([core, (core == owned_block).astype(jnp.int32), odd])
    side = jnp.pad(side, (0, members - 3))
    scal = jnp.stack(
        [shifts[:, 0], shifts[:, 1], live[order], side]
    ).astype(jnp.int32)

    rims = forward(radius, cut, scal, taps, est, inside, across)
    chunks, carries, main = [], [], None
    for i, (kept, packed) in enumerate(((kept_a, packed_a), (kept_b, packed_b))):
        runs = runs_of(half if i == 0 else 1, half, cut[i][1] - cut[i][0])
        mine, sib = pair_send(runs, kept, packed[-1], rims[-1:] if i == 0 else [main])
        is_first, is_last = i == 0, i == len(cut) - 1
        result = edges(
            radius, tile, is_first, is_last, runs, scal, taps, rims[i], mine, sib, carries
        )
        main, inside, across = result[:3]
        carries = result[3:]
        inside = lax.ppermute(inside, "joined", twin)
        across = lax.ppermute(across, "joined", other)
        chunks.append((main, inside, across))
    runs = runs_of(3, half, total_blocks)
    mine, sib = pair_send(runs, kept_c, packed_c[-1], [main, *chunks[0][1:]])
    mains = [chunk[0] for chunk in chunks]
    total = middle(radius, tile, runs, scal, taps, rims[-1], mine, sib, mains, *chunks[0][1:])
    out = update(radius, members, scal, total, est, *chunks[1][1:])
    return out[None]


def solution(mesh):
    return jax.shard_map(
        per_device,
        mesh=mesh,
        in_specs=(P("view", "joined", None), P("view", None, "joined", None), P(), P(), P()),
        out_specs=P("view", "joined", None),
        check_vma=False,
    )
```

```python
import functools

import jax
import jax.numpy as jnp
from jax import lax
from jax.experimental import pallas as pl
from jax.experimental.pallas import tpu as pltpu
from jax.sharding import PartitionSpec as P

MAXD = 16
BLOCKS = 2
LANES = 128
F32 = jnp.float32
BF16 = jnp.bfloat16
VMEM_LIMIT = 28 * 1024 * 1024


def split(x):
    hi = x.astype(BF16)
    return hi, (x - hi.astype(F32)).astype(BF16)


def mm(a, b):
    return jnp.dot(a, b, preferred_element_type=F32)


def slot_view(info, names, slot, half):
    core, block = info[names["core"]], info[names["block"]]
    other = slot >= half
    if isinstance(slot, int):
        side = 1 - core if other else core
        turn = slot % half
    else:
        side = jnp.where(other, 1 - core, core)
        turn = lax.rem(slot, half)
    step = jnp.where(side == block, 1, 0)
    return side * half + lax.rem(info[names["place"]] - turn - step + 2 * half, half)


def alive(info, names, lengths, slot, half):
    view = slot_view(info, names, slot, half)
    return jnp.where(info[names["row"]] < lengths[view, info[names["block"]]], 1.0, 0.0)


def toeplitz(row, rows, shift, width):
    turned = pltpu.roll(jnp.broadcast_to(row, (8, width)), lax.rem(shift + 4 * width, width), 1)
    wide = jnp.broadcast_to(turned[0:1], (rows, width))
    return pltpu.roll(wide, 0, 1, stride=1, stride_axis=0)


def side_by_side(left, right):
    hi, lo = split(jnp.concatenate([left, right], axis=1))
    return jnp.concatenate([hi, hi], axis=0), lo


def fetch(source, target, sem):
    copy = pltpu.make_async_copy(source, target, sem)
    copy.start()
    return copy


def fetch_sides(odd, inside, across, target, first_sem, second_sem):
    return [
        fetch(inside, target.at[1 - odd], first_sem),
        fetch(across, target.at[odd], second_sem),
    ]


def images(lhs, first, second, rows, blocks):
    part = mm(lhs[...], first) + mm(lhs[:, :LANES], second)
    result = []
    for j in range(blocks):
        n = (j + 1) % blocks
        here = part[j * rows : (j + 1) * rows, :LANES]
        result.append(here + part[n * rows : (n + 1) * rows, LANES:])
    return result


def spread(value, lhs):
    rows, cols = value.shape
    hi, lo = split(value)
    for j in range(cols // LANES):
        at = slice(j * LANES, (j + 1) * LANES)
        lhs[j * rows : (j + 1) * rows, :LANES] = hi[:, at]
        lhs[j * rows : (j + 1) * rows, LANES:] = lo[:, at]


def prepare_kernel(radius, names, info, offsets, lengths, psf, est, *refs):
    rim, fx, fy, fy_low, by, by_low, bx, bm, hi, lo, lhs, taps = refs
    slot = pl.program_id(0)
    half = rim.shape[0] // 2
    margin = radius + MAXD
    tile, cols = est.shape
    extended = tile + 2 * margin
    mid = tile - 2 * margin
    width = taps.shape[1]

    @pl.when(slot == 0)
    def _():
        hi[...], lo[...] = split(pltpu.roll(est[...], margin, 1))
        taps[...] = jnp.zeros(taps.shape, F32)

    view = slot_view(info, names, slot, half)
    dx, dy = offsets[view, 0], offsets[view, 1]
    weights = psf[view]
    taps[0:2, : 2 * radius + 1] = weights / jnp.sum(weights, axis=1, keepdims=True)
    gx, gy = taps[0:1, :], taps[1:2, :]
    band = toeplitz(gx, tile, dx + MAXD, width)
    back = jnp.transpose(band)[:extended, :]
    band = band[:, :extended]
    edge = jnp.concatenate([band[:margin], band[tile - margin :]], axis=0)
    fx[0] = jnp.concatenate(split(edge), axis=0)
    ahead = jnp.transpose(toeplitz(gy, LANES, dy + MAXD, width))
    fy[0], fy_low[0] = side_by_side(ahead[:LANES], ahead[LANES:])
    by[0], by_low[0] = side_by_side(
        toeplitz(gy, LANES, dy + MAXD - LANES, width)[:, :LANES],
        toeplitz(gy, LANES, dy + MAXD, width)[:, :LANES],
    )
    bx[...] = jnp.concatenate(split(back), axis=0)
    line = back[margin : margin + tile]
    wide = bm.shape[2]
    if wide > tile:
        line = jnp.concatenate([line, jnp.zeros((tile, wide - tile), F32)], axis=1)
    line = pltpu.roll(line, lax.rem(mid * slot - margin + wide, wide), 1)
    lane = lax.broadcasted_iota(jnp.int32, line.shape, 1)
    line = jnp.where((lane >= mid * slot) & (lane < mid * (slot + 1)), line, 0.0)
    bm[0] = jnp.concatenate(split(line), axis=0)

    b_hi, b_lo = split(band[margin : tile - margin, margin : margin + tile])
    both = mm(jnp.concatenate([b_hi, b_lo], axis=0), hi[...])
    spread(both[:mid] + both[mid:] + mm(b_hi, lo[...]), lhs)
    live = alive(info, names, lengths, slot, half)
    for j, image in enumerate(images(lhs, fy[0], fy_low[0], mid, cols // LANES)):
        rim[slot, :, j * LANES : (j + 1) * LANES] = live / image


def forward_kernel(radius, cut, names, info, lengths, est, across, inside, fx, fy, fy_low, *rest):
    outs, (e_hi, e_lo, lhs, halo, sems) = rest[:-5], rest[-5:]
    slot = pl.program_id(0)
    margin = radius + MAXD
    tile, cols = est.shape
    edge = 2 * margin

    @pl.when(slot == 0)
    def _():
        copies = fetch_sides(info[names["odd"]], inside, across, halo, sems.at[0], sems.at[1])
        for piece, at in ((est, margin), (halo.at[0], 0), (halo.at[1], margin + tile)):
            if at == 0:
                for copy in copies:
                    copy.wait()
            top, rest = split(pltpu.roll(piece[...], margin, 1))
            e_hi[at : at + piece.shape[0], :] = top
            e_lo[at : at + piece.shape[0], :] = rest

    live = alive(info, names, lengths, slot, outs[0].shape[0] // 2)
    both = mm(fx[0], e_hi[...])
    spread(both[:edge] + both[edge:] + mm(fx[0, :edge], e_lo[...]), lhs)
    for j, image in enumerate(images(lhs, fy[0], fy_low[0], edge, cols // LANES)):
        for out, (c0, c1) in zip(outs, cut):
            if c0 <= j < c1:
                out[slot, :, (j - c0) * LANES : (j - c0 + 1) * LANES] = live / image


def ratio_blurred(value, lhs, first, second):
    rows, cols = value.shape
    spread(value, lhs)
    part = mm(lhs[...], first) + mm(lhs[:, :LANES], second)
    return [part[j * rows : (j + 1) * rows] for j in range(cols // LANES)]


def runs_of(arrays, half, blocks):
    total = half * blocks
    marks = [round(total * i / arrays) for i in range(arrays + 1)]
    result = []
    for lo, hi in zip(marks, marks[1:]):
        runs = []
        for view in range(half):
            c0, c1 = max(lo, view * blocks), min(hi, (view + 1) * blocks)
            if c0 < c1:
                runs.append((view, c0 - view * blocks, c1 - view * blocks))
        result.append(runs)
    return result


def slot_values(slot, half, runs, mine, sib):
    if slot < half:
        return mine[slot][...]
    parts = []
    for ref, of_ref in zip(sib, runs):
        at = 0
        for view, c0, c1 in of_ref:
            width = (c1 - c0) * LANES
            if view == slot - half:
                parts.append(ref[:, at : at + width])
            at += width
    return parts[0] if len(parts) == 1 else jnp.concatenate(parts, axis=1)


def fetch_either(flag, source, other, target, sem):
    @pl.when(flag != 0)
    def _():
        fetch(other, target, sem)

    @pl.when(flag == 0)
    def _():
        fetch(source, target, sem)

    return pltpu.make_async_copy(source, target, sem)


def pair_kernel(half, runs, scal, *refs):
    kept, own, refs = refs[:half], refs[half], refs[half + 1 :]
    outs, sem = refs[-1 - len(runs) - half : -1], refs[-1]
    away, inner = scal[half], scal[half + 1]
    copies = []
    for out, of_out in zip(outs, runs):
        at = 0
        for view, c0, c1 in of_out:
            cols = slice(c0 * LANES, c1 * LANES)
            target = out.at[:, at : at + (c1 - c0) * LANES]
            place = (kept[view].at[away, :, cols], target, sem.at[len(copies)])
            if view < half - 1:
                copies.append(fetch(*place))
            else:
                copies.append(fetch_either(inner, place[0], own.at[away, :, cols], *place[1:]))
            at += (c1 - c0) * LANES
    for s, out in enumerate(outs[len(runs) :]):
        place = (kept[s].at[1 - away], out, sem.at[len(copies)])
        if s < half - 1:
            copies.append(fetch(*place))
        else:
            copies.append(fetch_either(inner, place[0], own.at[1 - away], *place[1:]))
    for copy in copies:
        copy.wait()


def edge_kernel(radius, tile, is_first, is_last, half, runs, names, scal, by, by_low, bx, rim, *rest):
    mine, rest = rest[:half], rest[half:]
    sib, rest = rest[: len(runs)], rest[len(runs) :]
    carries = []
    if not is_first:
        carries, rest = rest[: 1 + is_last], rest[1 + is_last :]
    main, across, inside = rest[:3]
    rest = rest[3:]
    if not is_last:
        (next_left, *rest) = rest
    if is_first and not is_last:
        (next_right, *rest) = rest
    lhs, s_hi, s_lo = rest
    slots = 2 * half
    margin = radius + MAXD
    extended = tile + 2 * margin
    for slot in range(slots):
        value = slot_values(slot, half, runs, mine, sib) * rim[slot]
        parts = ratio_blurred(value, lhs, by[slot], by_low[slot])
        lefts = [x[:, :LANES] for x in parts]
        rights = [x[:, LANES:] for x in parts]
        if not is_first:
            lefts = [carries[0][slot]] + lefts
        else:
            if is_last:
                closing = rights[0]
            else:
                next_right[slot] = rights[0]
            rights = rights[1:]
        if is_last:
            rights = rights + [closing if is_first else carries[1][slot]]
        else:
            next_left[slot] = lefts[-1]
            lefts = lefts[:-1]
        base = slot * tile
        for j, (left, right) in enumerate(zip(lefts, rights)):
            at = slice(j * LANES, (j + 1) * LANES)
            hi, lo = split(left + right)
            for ref, piece in ((s_hi, hi), (s_lo, lo)):
                ref[base : base + margin, at] = piece[:margin]
                ref[base + margin : base + tile - margin, at] = jnp.zeros((tile - 2 * margin, LANES), BF16)
                ref[base + tile - margin : base + tile, at] = piece[margin:]
    both = mm(bx[...], s_hi[...])
    total = both[:extended] + both[extended:] + mm(bx[:extended], s_lo[...])
    odd = scal[names["odd"]] != 0
    main[...] = total[margin : margin + tile]
    inside[...] = jnp.where(odd, total[:margin], total[margin + tile :])
    across[...] = jnp.where(odd, total[margin + tile :], total[:margin])


def middle_kernel(radius, tile, half, runs, names, scal, by, by_low, bm, rim, *rest):
    mine, rest = rest[:half], rest[half:]
    sib, rest = rest[: len(runs)], rest[len(runs) :]
    first, second, across, inside, total, lhs, s_hi, s_lo, part, edge, sems = rest
    width = first.shape[1]
    late = [
        fetch(first, part.at[:, :width], sems.at[0]),
        fetch(second, part.at[:, width:], sems.at[1]),
        *fetch_sides(scal[names["odd"]], inside, across, edge, sems.at[2], sems.at[3]),
    ]
    slots = 2 * half
    margin = radius + MAXD
    mid = tile - 2 * margin
    cols = total.shape[1]
    blocks = cols // LANES
    band = bm[0]
    for slot in range(1, slots):
        band = band + bm[slot]
    for slot in range(slots):
        value = slot_values(slot, half, runs, mine, sib) * rim[slot]
        parts = ratio_blurred(value, lhs, by[slot], by_low[slot])
        base = slot * mid
        for j in range(1, blocks + 1):
            at = slice((j - 1) * LANES, j * LANES)
            hi, lo = split(parts[j - 1][:, :LANES] + parts[j % blocks][:, LANES:])
            s_hi[base : base + mid, at] = hi
            s_lo[base : base + mid, at] = lo
    both = mm(band, s_hi[...])
    for copy in late:
        copy.wait()
    total[...] = both[:tile] + both[tile:] + mm(band[:tile], s_lo[...]) + part[...]
    total[:margin, :width] += edge[0]
    total[tile - margin :, :width] += edge[1]


def update_kernel(radius, tile, slots, names, scal, lengths, total, est, across, inside, out, edge, sems):
    margin = radius + MAXD
    copies = fetch_sides(scal[names["odd"]], inside, across, edge, sems.at[0], sems.at[1])
    count = alive(scal, names, lengths, 0, slots // 2)
    for slot in range(1, slots):
        count += alive(scal, names, lengths, slot, slots // 2)
    width, cols = inside.shape[1], est.shape[1]
    weight = 1.0 / jnp.full((1, cols), count, F32)
    for copy in copies:
        copy.wait()
    at = slice(cols - width, cols)
    total[:margin, at] += edge[0]
    total[tile - margin :, at] += edge[1]
    out[...] = est[...] * weight * pltpu.roll(total[...], LANES - margin, 1)


def light():
    return pl.CostEstimate(flops=0, bytes_accessed=1024, transcendentals=0)


def pack_kernel(starts, pieces, n_in, *refs):
    scal, refs = refs[0], refs[1:]
    ins, outs, sem = refs[:n_in], refs[n_in:-1], refs[-1]
    copies = []
    for i, (src, dst, start, src_at, dst_at) in enumerate(pieces):
        ref = ins[src]
        if start is not None and start < len(starts):
            ref = ref.at[pl.ds(scal[start], starts[start])]
        elif start is not None:
            ref = ref.at[pl.ds(pl.multiple_of(scal[start], 8), outs[dst].shape[0])]
        copies.append(fetch(ref.at[src_at], outs[dst].at[dst_at], sem.at[i]))
    for copy in copies:
        copy.wait()


def in_vmem():
    return pl.BlockSpec(memory_space=pltpu.VMEM)


def in_hbm():
    return pl.BlockSpec(memory_space=pltpu.HBM)


def anywhere():
    return pl.BlockSpec(memory_space=pl.ANY)


def from_vmem(operands):
    return [pltpu.with_memory_space_constraint(x, pltpu.VMEM) for x in operands]


def from_hbm(operands):
    return [pltpu.with_memory_space_constraint(x, pltpu.HBM) for x in operands]


def pack(scal, starts, ins, after, shapes, pieces, name):
    return pl.pallas_call(
        functools.partial(pack_kernel, starts, pieces, len(ins) + len(after)),
        grid_spec=pltpu.PrefetchScalarGridSpec(
            num_scalar_prefetch=1,
            grid=(1,),
            in_specs=[in_hbm()] * len(ins) + [anywhere()] * len(after),
            out_specs=[in_vmem()] * len(shapes),
            scratch_shapes=[pltpu.SemaphoreType.DMA((len(pieces),))],
        ),
        out_shape=[jax.ShapeDtypeStruct(s, F32) for s in shapes],
        compiler_params=params(),
        cost_estimate=light(),
        name=name,
    )(scal, *from_hbm(ins), *after)


def part_pair(scal, runs, kept, own, after):
    half = len(kept)
    rows = own.shape[1]
    shapes = [(rows, sum(c1 - c0 for _, c0, c1 in of) * LANES) for of in runs]
    shapes += [(rows, own.shape[2])] * half
    out = pl.pallas_call(
        functools.partial(pair_kernel, half, runs),
        grid_spec=pltpu.PrefetchScalarGridSpec(
            num_scalar_prefetch=1,
            grid=(1,),
            in_specs=[in_hbm()] * (half + 1) + [anywhere()] * len(after),
            out_specs=[in_vmem()] * len(shapes),
            scratch_shapes=[pltpu.SemaphoreType.DMA((half + sum(len(of) for of in runs),))],
        ),
        out_shape=[jax.ShapeDtypeStruct(s, F32) for s in shapes],
        compiler_params=params(),
        cost_estimate=light(),
        name="pair",
    )(scal, *from_hbm([*kept, own]), *after)
    return out[: len(runs)], out[len(runs) :]


def whole_spec(shape):
    return pl.BlockSpec(shape, lambda i, *_: (0,) * len(shape))


def params():
    return pltpu.CompilerParams(vmem_limit_bytes=VMEM_LIMIT, dimension_semantics=("arbitrary",))


def prepare(radius, names, info, offsets, lengths, psf, est):
    slots = psf.shape[0]
    tile, cols = est.shape
    margin = radius + MAXD
    mid, extended = tile - 2 * margin, tile + 2 * margin
    bands = [
        (slots, 4 * margin, extended),
        (slots, 2 * LANES, 2 * LANES),
        (slots, LANES, 2 * LANES),
        (slots, 2 * LANES, 2 * LANES),
        (slots, LANES, 2 * LANES),
        (2 * extended, slots * tile),
        (slots, 2 * tile, slots * mid),
    ]
    specs = [pl.BlockSpec((1,) + s[1:], lambda i, *_: (i, 0, 0)) for s in bands]
    specs[5] = pl.BlockSpec((2 * extended, tile), lambda i, *_: (0, i))
    return pl.pallas_call(
        functools.partial(prepare_kernel, radius, names),
        grid_spec=pltpu.PrefetchScalarGridSpec(
            num_scalar_prefetch=3,
            grid=(slots,),
            in_specs=[whole_spec(psf.shape), in_vmem()],
            out_specs=[in_vmem()] + specs,
            scratch_shapes=[
                pltpu.VMEM((tile, cols), BF16),
                pltpu.VMEM((tile, cols), BF16),
                pltpu.VMEM((mid * cols // LANES, 2 * LANES), BF16),
                pltpu.VMEM((8, 2 * LANES), F32),
            ],
        ),
        out_shape=[jax.ShapeDtypeStruct((slots, mid, cols), F32)]
        + [jax.ShapeDtypeStruct(s, BF16) for s in bands],
        compiler_params=params(),
        cost_estimate=light(),
        name="prepare",
    )(info, offsets, lengths, psf, *from_vmem([est]))


def forward(radius, cut, names, info, lengths, est, across, inside, fx, fy, fy_low):
    slots = fx.shape[0]
    tile, cols = est.shape
    margin = radius + MAXD
    shapes = [(slots, 2 * margin, (c1 - c0) * LANES) for c0, c1 in cut]
    extended = tile + 2 * margin
    return pl.pallas_call(
        functools.partial(forward_kernel, radius, cut, names),
        grid_spec=pltpu.PrefetchScalarGridSpec(
            num_scalar_prefetch=2,
            grid=(slots,),
            in_specs=[in_vmem(), in_hbm(), in_hbm()]
            + [pl.BlockSpec((1,) + x.shape[1:], lambda i, *_: (i, 0, 0)) for x in (fx, fy, fy_low)],
            out_specs=[in_vmem()] * len(shapes),
            scratch_shapes=[
                pltpu.VMEM((extended, cols), BF16),
                pltpu.VMEM((extended, cols), BF16),
                pltpu.VMEM((2 * margin * cols // LANES, 2 * LANES), BF16),
                pltpu.VMEM((2, margin, cols), F32),
                pltpu.SemaphoreType.DMA((2,)),
            ],
        ),
        out_shape=[jax.ShapeDtypeStruct(s, F32) for s in shapes],
        compiler_params=params(),
        cost_estimate=light(),
        name="forward",
    )(info, lengths, *from_vmem([est]), *from_hbm([across, inside]), fx, fy, fy_low)


def edges(radius, tile, is_first, is_last, runs, names, scal, bands, rim, mine, sib, carries):
    half = len(mine)
    slots = 2 * half
    margin = radius + MAXD
    blocks = rim.shape[2] // LANES
    made = (blocks - (1 if is_first else 0) + (1 if is_last else 0)) * LANES
    shapes = [(tile, made), (margin, made), (margin, made)]
    carried = (slots, 2 * margin, LANES)
    if not is_last:
        shapes.append(carried)
        if is_first:
            shapes.append(carried)
    return pl.pallas_call(
        functools.partial(edge_kernel, radius, tile, is_first, is_last, half, runs, names),
        grid_spec=pltpu.PrefetchScalarGridSpec(
            num_scalar_prefetch=1,
            grid=(1,),
            in_specs=[in_vmem()] * (4 + half + len(sib) + len(carries)),
            out_specs=[in_vmem()] * len(shapes),
            scratch_shapes=[
                pltpu.VMEM((blocks * 2 * margin, 2 * LANES), BF16),
                pltpu.VMEM((slots * tile, made), BF16),
                pltpu.VMEM((slots * tile, made), BF16),
            ],
        ),
        out_shape=[jax.ShapeDtypeStruct(s, F32) for s in shapes],
        compiler_params=params(),
        cost_estimate=light(),
        name="edges",
    )(scal, *from_vmem([*bands, rim, *mine, *sib, *carries]))


def middle(radius, tile, runs, names, scal, bands, rim, mine, sib, mains, inside, across):
    half = len(mine)
    slots, mid, cols = rim.shape
    margin = radius + MAXD
    return pl.pallas_call(
        functools.partial(middle_kernel, radius, tile, half, runs, names),
        grid_spec=pltpu.PrefetchScalarGridSpec(
            num_scalar_prefetch=1,
            grid=(1,),
            in_specs=[in_vmem()] * (4 + half + len(runs))
            + [anywhere()] * 4,
            out_specs=in_vmem(),
            scratch_shapes=[
                pltpu.VMEM((cols // LANES * mid, 2 * LANES), BF16),
                pltpu.VMEM((slots * mid, cols), BF16),
                pltpu.VMEM((slots * mid, cols), BF16),
                pltpu.VMEM((tile, cols), F32),
                pltpu.VMEM((2,) + inside.shape, F32),
                pltpu.SemaphoreType.DMA((4,)),
            ],
        ),
        out_shape=jax.ShapeDtypeStruct((tile, cols), F32),
        compiler_params=params(),
        cost_estimate=light(),
        name="middle",
    )(scal, *from_vmem([*bands, rim, *mine, *sib]), *mains, across, inside)


def update(radius, slots, names, info, lengths, total, est, inside, across):
    tile = est.shape[0]
    return pl.pallas_call(
        functools.partial(update_kernel, radius, tile, slots, names),
        grid_spec=pltpu.PrefetchScalarGridSpec(
            num_scalar_prefetch=2,
            grid=(1,),
            in_specs=[in_vmem()] * 2 + [anywhere()] * 2,
            out_specs=whole_spec(est.shape),
            scratch_shapes=[
                pltpu.VMEM((2,) + inside.shape, F32),
                pltpu.SemaphoreType.DMA((2,)),
            ],
        ),
        out_shape=jax.ShapeDtypeStruct(est.shape, F32),
        compiler_params=params(),
        cost_estimate=light(),
        name="update",
    )(info, lengths, *from_vmem([total, est]), across, inside)


def per_device(estimate, views, psf, offsets, lengths):
    size = lax.axis_size("view")
    joined = lax.axis_size("joined")
    position = lax.axis_index("view")
    members = size // BLOCKS
    half = members // 2
    member, block = position // BLOCKS, position % BLOCKS
    planes, tile, cols = views.shape[1:]
    radius = (psf.shape[2] - 1) // 2
    margin = radius + MAXD
    stack = views[0]
    est = estimate[0]
    total_blocks = cols // LANES

    odd = lax.axis_index("joined") % 2
    twin = [(i, i ^ 1) for i in range(joined)]
    other = [(i, (i - 1 if i % 2 == 0 else i + 1) % joined) for i in range(joined)]

    def target(p, s):
        k, b = p // BLOCKS, p % BLOCKS
        t = (k % half + s + (1 if k // half == b else 0)) % half
        return 2 * (b * half + t) + k // half

    first = total_blocks * 8 // 16
    cut = ((0, first), (first, total_blocks))
    away = [
        2 * ((member % half + s + (member // half == block).astype(jnp.int32)) % half)
        for s in range(half)
    ]
    inner = (member // half == block).astype(jnp.int32)
    edge_at = (1 - odd) * (tile - margin)
    away = away + [1 - position % 2, inner, edge_at, tile - margin - edge_at]
    pair, core = position // 2, position % 2
    extra = {
        "odd": odd, "core": core, "block": pair // half, "place": pair % half,
        "row": position % planes,
    }
    names = {name: len(away) + i for i, name in enumerate(extra)}
    away = jnp.stack(away + list(extra.values())).astype(jnp.int32)
    starts = (2,) * half + (1,)
    top, bottom = slice(0, margin), slice(tile - margin, tile)
    low, high = slice(0, margin), slice(margin, 2 * margin)
    every = slice(None)

    def edge_pieces(c0, c1):
        at = slice(c0 * LANES, c1 * LANES)
        pieces = []
        for s in range(half):
            pieces.append((0, s, s, (every, top, at), (every, low)))
            pieces.append((0, s, s, (every, bottom, at), (every, high)))
        return pieces

    def view_send(parts):
        sent = []
        for s, x in enumerate(parts):
            pairs = [(p, target(p, s)) for p in range(size)]
            sent.append(lax.ppermute(x, "view", [(p, q) for p, q in pairs if p != q]))
        return sent

    def pair_send(runs, kept, own, after):
        others, mine = part_pair(away, runs, kept, own, after)
        return mine, [lax.ppermute(x, "view", [(p, p ^ 1) for p in range(size)]) for x in others]

    def edge_shape(c0, c1):
        return (2, 2 * margin, (c1 - c0) * LANES)

    packed_a = pack(
        away, starts, [stack], [], [edge_shape(*cut[0])] * half, edge_pieces(*cut[0]), "pack_first"
    )
    slab = pack(
        away, starts, [est], packed_a[:1], [(margin, cols)] * 2,
        [
            (0, 0, half + 2, (every,), (every,)),
            (0, 1, half + 3, (every,), (every,)),
        ],
        "pack_slab",
    )
    across = lax.ppermute(slab[1], "joined", other)
    inside = lax.ppermute(slab[0], "joined", twin)
    kept_a = view_send(packed_a)
    center = slice(margin, tile - margin)
    packed = pack(
        away, starts, [stack], slab[:1],
        [edge_shape(*cut[1])] * half + [(2, tile - 2 * margin, cols)] * half,
        edge_pieces(*cut[1])
        + [(0, half + s, s, (every, center), (every,)) for s in range(half)],
        "pack_second",
    )
    rim_middle, fx, fy, fy_low, by, by_low, bx, bm = prepare(
        radius, names, away, offsets, lengths, psf, est
    )
    packed_b, packed_c = list(packed[:half]), packed[half:]
    fellow = [(p, p ^ 1) for p in range(size)]
    runs_a, runs_b = [
        runs_of(arrays, half, c1 - c0) for arrays, (c0, c1) in zip((2, 1), cut)
    ]
    others, mine_a = part_pair(away, runs_a, kept_a, packed_a[-1], [rim_middle])
    others = list(others)
    packed_b[0], across, inside, others[0] = lax.optimization_barrier(
        (packed_b[0], across, inside, others[0])
    )
    sib_a = [lax.ppermute(x, "view", fellow) for x in others]
    kept_b = view_send(packed_b)
    kept_c = view_send(packed_c)
    rims = forward(radius, cut, names, away, lengths, est, across, inside, fx, fy, fy_low)
    main, across, inside, *carries = edges(
        radius, tile, True, False, runs_a, names, away, (by, by_low, bx), rims[0], mine_a, sib_a, []
    )
    across = lax.ppermute(across, "joined", other)
    inside = lax.ppermute(inside, "joined", twin)
    chunks = [(main, inside, across)]
    mine, sib = pair_send(runs_b, kept_b, packed_b[-1], [main])
    main, across, inside = edges(
        radius, tile, False, True, runs_b, names, away, (by, by_low, bx), rims[1], mine, sib, carries
    )
    across = lax.ppermute(across, "joined", other)
    inside = lax.ppermute(inside, "joined", twin)
    chunks.append((main, inside, across))
    runs = runs_of(3, half, total_blocks)
    mine, sib = pair_send(runs, kept_c, packed_c[-1], [main, chunks[0][2], chunks[0][1]])
    mains = [chunk[0] for chunk in chunks]
    bands = (by, by_low, bm)
    total = middle(radius, tile, runs, names, away, bands, rim_middle, mine, sib, mains, *chunks[0][1:])
    out = update(radius, members, names, away, lengths, total, est, *chunks[1][1:])
    return out[None]


def solution(mesh):
    return jax.shard_map(
        per_device,
        mesh=mesh,
        in_specs=(P("view", "joined", None), P("view", None, "joined", None), P(), P(), P()),
        out_specs=P("view", "joined", None),
        check_vma=False,
    )
```

```python
import functools

import jax
import jax.numpy as jnp
from jax import lax
from jax.experimental import pallas as pl
from jax.experimental.pallas import tpu as pltpu
from jax.sharding import PartitionSpec as P

MAXD = 16
BLOCKS = 2
LANES = 128
F32 = jnp.float32
BF16 = jnp.bfloat16
VMEM_LIMIT = 28 * 1024 * 1024


def split(x):
    hi = x.astype(BF16)
    return hi, (x - hi.astype(F32)).astype(BF16)


def mm(a, b):
    return jnp.dot(a, b, preferred_element_type=F32)


def slot_view(info, names, slot, half):
    core, block = info[names["core"]], info[names["block"]]
    other = slot >= half
    if isinstance(slot, int):
        side = 1 - core if other else core
        turn = slot % half
    else:
        side = jnp.where(other, 1 - core, core)
        turn = lax.rem(slot, half)
    step = jnp.where(side == block, 1, 0)
    return side * half + lax.rem(info[names["place"]] - turn - step + 2 * half, half)


def alive(info, names, lengths, slot, half):
    view = slot_view(info, names, slot, half)
    return jnp.where(info[names["row"]] < lengths[view, info[names["block"]]], 1.0, 0.0)


def toeplitz(row, rows, shift, width):
    turned = pltpu.roll(jnp.broadcast_to(row, (8, width)), lax.rem(shift + 4 * width, width), 1)
    wide = jnp.broadcast_to(turned[0:1], (rows, width))
    return pltpu.roll(wide, 0, 1, stride=1, stride_axis=0)


def side_by_side(left, right):
    hi, lo = split(jnp.concatenate([left, right], axis=1))
    return jnp.concatenate([hi, hi], axis=0), lo


def fetch(source, target, sem):
    copy = pltpu.make_async_copy(source, target, sem)
    copy.start()
    return copy


def fetch_sides(odd, inside, across, target, first_sem, second_sem):
    return [
        fetch(inside, target.at[1 - odd], first_sem),
        fetch(across, target.at[odd], second_sem),
    ]


def images(lhs, first, second, rows, blocks):
    part = mm(lhs[...], first) + mm(lhs[:, :LANES], second)
    result = []
    for j in range(blocks):
        n = (j + 1) % blocks
        here = part[j * rows : (j + 1) * rows, :LANES]
        result.append(here + part[n * rows : (n + 1) * rows, LANES:])
    return result


def spread(value, lhs):
    rows, cols = value.shape
    hi, lo = split(value)
    for j in range(cols // LANES):
        at = slice(j * LANES, (j + 1) * LANES)
        lhs[j * rows : (j + 1) * rows, :LANES] = hi[:, at]
        lhs[j * rows : (j + 1) * rows, LANES:] = lo[:, at]


def prepare_kernel(radius, names, info, offsets, lengths, psf, est, *refs):
    rim, fx, fy, fy_low, by, by_low, bx, bm, hi, lo, lhs, taps = refs
    slot = pl.program_id(0)
    half = rim.shape[0] // 2
    margin = radius + MAXD
    tile, cols = est.shape
    extended = tile + 2 * margin
    mid = tile - 2 * margin
    width = taps.shape[1]

    @pl.when(slot == 0)
    def _():
        hi[...], lo[...] = split(pltpu.roll(est[...], margin, 1))
        taps[...] = jnp.zeros(taps.shape, F32)

    view = slot_view(info, names, slot, half)
    dx, dy = offsets[view, 0], offsets[view, 1]
    weights = psf[view]
    taps[0:2, : 2 * radius + 1] = weights / jnp.sum(weights, axis=1, keepdims=True)
    gx, gy = taps[0:1, :], taps[1:2, :]
    band = toeplitz(gx, tile, dx + MAXD, width)
    back = jnp.transpose(band)[:extended, :]
    band = band[:, :extended]
    edge = jnp.concatenate([band[:margin], band[tile - margin :]], axis=0)
    fx[0] = jnp.concatenate(split(edge), axis=0)
    ahead = jnp.transpose(toeplitz(gy, LANES, dy + MAXD, width))
    fy[0], fy_low[0] = side_by_side(ahead[:LANES], ahead[LANES:])
    by[0], by_low[0] = side_by_side(
        toeplitz(gy, LANES, dy + MAXD - LANES, width)[:, :LANES],
        toeplitz(gy, LANES, dy + MAXD, width)[:, :LANES],
    )
    bx[...] = jnp.concatenate(split(back), axis=0)
    line = back[margin : margin + tile]
    wide = bm.shape[2]
    if wide > tile:
        line = jnp.concatenate([line, jnp.zeros((tile, wide - tile), F32)], axis=1)
    line = pltpu.roll(line, lax.rem(mid * slot - margin + wide, wide), 1)
    lane = lax.broadcasted_iota(jnp.int32, line.shape, 1)
    line = jnp.where((lane >= mid * slot) & (lane < mid * (slot + 1)), line, 0.0)
    bm[0] = jnp.concatenate(split(line), axis=0)

    b_hi, b_lo = split(band[margin : tile - margin, margin : margin + tile])
    both = mm(jnp.concatenate([b_hi, b_lo], axis=0), hi[...])
    spread(both[:mid] + both[mid:] + mm(b_hi, lo[...]), lhs)
    live = alive(info, names, lengths, slot, half)
    for j, image in enumerate(images(lhs, fy[0], fy_low[0], mid, cols // LANES)):
        rim[slot, :, j * LANES : (j + 1) * LANES] = live / image


def forward_kernel(radius, cut, names, info, lengths, est, across, inside, fx, fy, fy_low, *rest):
    outs, (e_hi, e_lo, lhs, halo, sems) = rest[:-5], rest[-5:]
    slot = pl.program_id(0)
    margin = radius + MAXD
    tile, cols = est.shape
    edge = 2 * margin

    @pl.when(slot == 0)
    def _():
        copies = fetch_sides(info[names["odd"]], inside, across, halo, sems.at[0], sems.at[1])
        for piece, at in ((est, margin), (halo.at[0], 0), (halo.at[1], margin + tile)):
            if at == 0:
                for copy in copies:
                    copy.wait()
            top, rest = split(pltpu.roll(piece[...], margin, 1))
            e_hi[at : at + piece.shape[0], :] = top
            e_lo[at : at + piece.shape[0], :] = rest

    live = alive(info, names, lengths, slot, outs[0].shape[0] // 2)
    both = mm(fx[0], e_hi[...])
    spread(both[:edge] + both[edge:] + mm(fx[0, :edge], e_lo[...]), lhs)
    for j, image in enumerate(images(lhs, fy[0], fy_low[0], edge, cols // LANES)):
        for out, (c0, c1) in zip(outs, cut):
            if c0 <= j < c1:
                out[slot, :, (j - c0) * LANES : (j - c0 + 1) * LANES] = live / image


def ratio_blurred(value, lhs, first, second):
    rows, cols = value.shape
    spread(value, lhs)
    part = mm(lhs[...], first) + mm(lhs[:, :LANES], second)
    return [part[j * rows : (j + 1) * rows] for j in range(cols // LANES)]


def runs_of(arrays, half, blocks):
    total = half * blocks
    marks = [round(total * i / arrays) for i in range(arrays + 1)]
    result = []
    for lo, hi in zip(marks, marks[1:]):
        runs = []
        for view in range(half):
            c0, c1 = max(lo, view * blocks), min(hi, (view + 1) * blocks)
            if c0 < c1:
                runs.append((view, c0 - view * blocks, c1 - view * blocks))
        result.append(runs)
    return result


def slot_values(slot, half, runs, mine, sib):
    if slot < half:
        return mine[slot][...]
    parts = []
    for ref, of_ref in zip(sib, runs):
        at = 0
        for view, c0, c1 in of_ref:
            width = (c1 - c0) * LANES
            if view == slot - half:
                parts.append(ref[:, at : at + width])
            at += width
    return parts[0] if len(parts) == 1 else jnp.concatenate(parts, axis=1)


def fetch_either(flag, source, other, target, sem):
    @pl.when(flag != 0)
    def _():
        fetch(other, target, sem)

    @pl.when(flag == 0)
    def _():
        fetch(source, target, sem)

    return pltpu.make_async_copy(source, target, sem)


def pair_kernel(half, runs, scal, *refs):
    kept, own, refs = refs[:half], refs[half], refs[half + 1 :]
    outs, sem = refs[-1 - len(runs) - half : -1], refs[-1]
    away, inner = scal[half], scal[half + 1]
    copies = []
    for out, of_out in zip(outs, runs):
        at = 0
        for view, c0, c1 in of_out:
            cols = slice(c0 * LANES, c1 * LANES)
            target = out.at[:, at : at + (c1 - c0) * LANES]
            place = (kept[view].at[away, :, cols], target, sem.at[len(copies)])
            if view < half - 1:
                copies.append(fetch(*place))
            else:
                copies.append(fetch_either(inner, place[0], own.at[away, :, cols], *place[1:]))
            at += (c1 - c0) * LANES
    for s, out in enumerate(outs[len(runs) :]):
        place = (kept[s].at[1 - away], out, sem.at[len(copies)])
        if s < half - 1:
            copies.append(fetch(*place))
        else:
            copies.append(fetch_either(inner, place[0], own.at[1 - away], *place[1:]))
    for copy in copies:
        copy.wait()


def edge_kernel(radius, tile, is_first, is_last, half, runs, names, scal, by, by_low, bx, rim, *rest):
    mine, rest = rest[:half], rest[half:]
    sib, rest = rest[: len(runs)], rest[len(runs) :]
    carries = []
    if not is_first:
        carries, rest = rest[: 1 + is_last], rest[1 + is_last :]
    main, across, inside = rest[:3]
    rest = rest[3:]
    if not is_last:
        (next_left, *rest) = rest
    if is_first and not is_last:
        (next_right, *rest) = rest
    lhs, s_hi, s_lo = rest
    slots = 2 * half
    margin = radius + MAXD
    extended = tile + 2 * margin
    for slot in range(slots):
        value = slot_values(slot, half, runs, mine, sib) * rim[slot]
        parts = ratio_blurred(value, lhs, by[slot], by_low[slot])
        lefts = [x[:, :LANES] for x in parts]
        rights = [x[:, LANES:] for x in parts]
        if not is_first:
            lefts = [carries[0][slot]] + lefts
        else:
            if is_last:
                closing = rights[0]
            else:
                next_right[slot] = rights[0]
            rights = rights[1:]
        if is_last:
            rights = rights + [closing if is_first else carries[1][slot]]
        else:
            next_left[slot] = lefts[-1]
            lefts = lefts[:-1]
        base = slot * tile
        for j, (left, right) in enumerate(zip(lefts, rights)):
            at = slice(j * LANES, (j + 1) * LANES)
            hi, lo = split(left + right)
            for ref, piece in ((s_hi, hi), (s_lo, lo)):
                ref[base : base + margin, at] = piece[:margin]
                ref[base + margin : base + tile - margin, at] = jnp.zeros((tile - 2 * margin, LANES), BF16)
                ref[base + tile - margin : base + tile, at] = piece[margin:]
    both = mm(bx[...], s_hi[...])
    total = both[:extended] + both[extended:] + mm(bx[:extended], s_lo[...])
    odd = scal[names["odd"]] != 0
    main[...] = total[margin : margin + tile]
    inside[...] = jnp.where(odd, total[:margin], total[margin + tile :])
    across[...] = jnp.where(odd, total[margin + tile :], total[:margin])


def middle_kernel(radius, tile, half, runs, names, scal, by, by_low, bm, rim, *rest):
    mine, rest = rest[:half], rest[half:]
    sib, rest = rest[: len(runs)], rest[len(runs) :]
    first, second, across, inside, total, lhs, s_hi, s_lo, part, edge, sems = rest
    width = first.shape[1]
    late = [
        fetch(first, part.at[:, :width], sems.at[0]),
        fetch(second, part.at[:, width:], sems.at[1]),
        *fetch_sides(scal[names["odd"]], inside, across, edge, sems.at[2], sems.at[3]),
    ]
    slots = 2 * half
    margin = radius + MAXD
    mid = tile - 2 * margin
    cols = total.shape[1]
    blocks = cols // LANES
    band = bm[0]
    for slot in range(1, slots):
        band = band + bm[slot]
    for slot in range(slots):
        value = slot_values(slot, half, runs, mine, sib) * rim[slot]
        parts = ratio_blurred(value, lhs, by[slot], by_low[slot])
        base = slot * mid
        for j in range(1, blocks + 1):
            at = slice((j - 1) * LANES, j * LANES)
            hi, lo = split(parts[j - 1][:, :LANES] + parts[j % blocks][:, LANES:])
            s_hi[base : base + mid, at] = hi
            s_lo[base : base + mid, at] = lo
    both = mm(band, s_hi[...])
    for copy in late:
        copy.wait()
    total[...] = both[:tile] + both[tile:] + mm(band[:tile], s_lo[...]) + part[...]
    total[:margin, :width] += edge[0]
    total[tile - margin :, :width] += edge[1]


def add_rows(total, first, rows, margin, start):
    tile = total.shape[0]
    at = slice(start, start + rows.shape[1])

    @pl.when(first)
    def _():
        total[:margin, at] += rows[...]

    @pl.when(jnp.logical_not(first))
    def _():
        total[tile - margin :, at] += rows[...]


def update_kernel(radius, tile, slots, names, scal, lengths, total, est, across, inside, out):
    margin = radius + MAXD
    count = alive(scal, names, lengths, 0, slots // 2)
    for slot in range(1, slots):
        count += alive(scal, names, lengths, slot, slots // 2)
    width, cols = inside.shape[1], est.shape[1]
    weight = 1.0 / jnp.full((1, cols), count, F32)
    even = scal[names["odd"]] == 0
    add_rows(total, even, across, margin, cols - width)
    add_rows(total, jnp.logical_not(even), inside, margin, cols - width)
    out[...] = est[...] * weight * pltpu.roll(total[...], LANES - margin, 1)


def light():
    return pl.CostEstimate(flops=0, bytes_accessed=1024, transcendentals=0)


def pack_kernel(starts, pieces, n_in, *refs):
    scal, refs = refs[0], refs[1:]
    ins, outs, sem = refs[:n_in], refs[n_in:-1], refs[-1]
    copies = []
    for i, (src, dst, start, src_at, dst_at) in enumerate(pieces):
        ref = ins[src]
        if start is not None and start < len(starts):
            ref = ref.at[pl.ds(scal[start], starts[start])]
        elif start is not None:
            ref = ref.at[pl.ds(pl.multiple_of(scal[start], 8), outs[dst].shape[0])]
        copies.append(fetch(ref.at[src_at], outs[dst].at[dst_at], sem.at[i]))
    for copy in copies:
        copy.wait()


def in_vmem():
    return pl.BlockSpec(memory_space=pltpu.VMEM)


def in_hbm():
    return pl.BlockSpec(memory_space=pltpu.HBM)


def anywhere():
    return pl.BlockSpec(memory_space=pl.ANY)


def from_vmem(operands):
    return [pltpu.with_memory_space_constraint(x, pltpu.VMEM) for x in operands]


def from_hbm(operands):
    return [pltpu.with_memory_space_constraint(x, pltpu.HBM) for x in operands]


def pack(scal, starts, ins, after, shapes, pieces, name):
    return pl.pallas_call(
        functools.partial(pack_kernel, starts, pieces, len(ins) + len(after)),
        grid_spec=pltpu.PrefetchScalarGridSpec(
            num_scalar_prefetch=1,
            grid=(1,),
            in_specs=[in_hbm()] * len(ins) + [anywhere()] * len(after),
            out_specs=[in_vmem()] * len(shapes),
            scratch_shapes=[pltpu.SemaphoreType.DMA((len(pieces),))],
        ),
        out_shape=[jax.ShapeDtypeStruct(s, F32) for s in shapes],
        compiler_params=params(),
        cost_estimate=light(),
        name=name,
    )(scal, *from_hbm(ins), *after)


def part_pair(scal, runs, kept, own, after):
    half = len(kept)
    rows = own.shape[1]
    shapes = [(rows, sum(c1 - c0 for _, c0, c1 in of) * LANES) for of in runs]
    shapes += [(rows, own.shape[2])] * half
    out = pl.pallas_call(
        functools.partial(pair_kernel, half, runs),
        grid_spec=pltpu.PrefetchScalarGridSpec(
            num_scalar_prefetch=1,
            grid=(1,),
            in_specs=[in_hbm()] * (half + 1) + [anywhere()] * len(after),
            out_specs=[in_vmem()] * len(shapes),
            scratch_shapes=[pltpu.SemaphoreType.DMA((half + sum(len(of) for of in runs),))],
        ),
        out_shape=[jax.ShapeDtypeStruct(s, F32) for s in shapes],
        compiler_params=params(),
        cost_estimate=light(),
        name="pair",
    )(scal, *from_hbm([*kept, own]), *after)
    return out[: len(runs)], out[len(runs) :]


def whole_spec(shape):
    return pl.BlockSpec(shape, lambda i, *_: (0,) * len(shape))


def params():
    return pltpu.CompilerParams(vmem_limit_bytes=VMEM_LIMIT, dimension_semantics=("arbitrary",))


def prepare(radius, names, info, offsets, lengths, psf, est):
    slots = psf.shape[0]
    tile, cols = est.shape
    margin = radius + MAXD
    mid, extended = tile - 2 * margin, tile + 2 * margin
    bands = [
        (slots, 4 * margin, extended),
        (slots, 2 * LANES, 2 * LANES),
        (slots, LANES, 2 * LANES),
        (slots, 2 * LANES, 2 * LANES),
        (slots, LANES, 2 * LANES),
        (2 * extended, slots * tile),
        (slots, 2 * tile, slots * mid),
    ]
    specs = [pl.BlockSpec((1,) + s[1:], lambda i, *_: (i, 0, 0)) for s in bands]
    specs[5] = pl.BlockSpec((2 * extended, tile), lambda i, *_: (0, i))
    return pl.pallas_call(
        functools.partial(prepare_kernel, radius, names),
        grid_spec=pltpu.PrefetchScalarGridSpec(
            num_scalar_prefetch=3,
            grid=(slots,),
            in_specs=[whole_spec(psf.shape), in_vmem()],
            out_specs=[in_vmem()] + specs,
            scratch_shapes=[
                pltpu.VMEM((tile, cols), BF16),
                pltpu.VMEM((tile, cols), BF16),
                pltpu.VMEM((mid * cols // LANES, 2 * LANES), BF16),
                pltpu.VMEM((8, 2 * LANES), F32),
            ],
        ),
        out_shape=[jax.ShapeDtypeStruct((slots, mid, cols), F32)]
        + [jax.ShapeDtypeStruct(s, BF16) for s in bands],
        compiler_params=params(),
        cost_estimate=light(),
        name="prepare",
    )(info, offsets, lengths, psf, *from_vmem([est]))


def forward(radius, cut, names, info, lengths, est, across, inside, fx, fy, fy_low):
    slots = fx.shape[0]
    tile, cols = est.shape
    margin = radius + MAXD
    shapes = [(slots, 2 * margin, (c1 - c0) * LANES) for c0, c1 in cut]
    extended = tile + 2 * margin
    return pl.pallas_call(
        functools.partial(forward_kernel, radius, cut, names),
        grid_spec=pltpu.PrefetchScalarGridSpec(
            num_scalar_prefetch=2,
            grid=(slots,),
            in_specs=[in_vmem(), in_hbm(), in_hbm()]
            + [pl.BlockSpec((1,) + x.shape[1:], lambda i, *_: (i, 0, 0)) for x in (fx, fy, fy_low)],
            out_specs=[in_vmem()] * len(shapes),
            scratch_shapes=[
                pltpu.VMEM((extended, cols), BF16),
                pltpu.VMEM((extended, cols), BF16),
                pltpu.VMEM((2 * margin * cols // LANES, 2 * LANES), BF16),
                pltpu.VMEM((2, margin, cols), F32),
                pltpu.SemaphoreType.DMA((2,)),
            ],
        ),
        out_shape=[jax.ShapeDtypeStruct(s, F32) for s in shapes],
        compiler_params=params(),
        cost_estimate=light(),
        name="forward",
    )(info, lengths, *from_vmem([est]), *from_hbm([across, inside]), fx, fy, fy_low)


def edges(radius, tile, is_first, is_last, runs, names, scal, bands, rim, mine, sib, carries):
    half = len(mine)
    slots = 2 * half
    margin = radius + MAXD
    blocks = rim.shape[2] // LANES
    made = (blocks - (1 if is_first else 0) + (1 if is_last else 0)) * LANES
    shapes = [(tile, made), (margin, made), (margin, made)]
    carried = (slots, 2 * margin, LANES)
    if not is_last:
        shapes.append(carried)
        if is_first:
            shapes.append(carried)
    return pl.pallas_call(
        functools.partial(edge_kernel, radius, tile, is_first, is_last, half, runs, names),
        grid_spec=pltpu.PrefetchScalarGridSpec(
            num_scalar_prefetch=1,
            grid=(1,),
            in_specs=[in_vmem()] * (4 + half + len(sib) + len(carries)),
            out_specs=[in_vmem()] * len(shapes),
            scratch_shapes=[
                pltpu.VMEM((blocks * 2 * margin, 2 * LANES), BF16),
                pltpu.VMEM((slots * tile, made), BF16),
                pltpu.VMEM((slots * tile, made), BF16),
            ],
        ),
        out_shape=[jax.ShapeDtypeStruct(s, F32) for s in shapes],
        compiler_params=params(),
        cost_estimate=light(),
        name="edges",
    )(scal, *from_vmem([*bands, rim, *mine, *sib, *carries]))


def middle(radius, tile, runs, names, scal, bands, rim, mine, sib, mains, inside, across):
    half = len(mine)
    slots, mid, cols = rim.shape
    margin = radius + MAXD
    return pl.pallas_call(
        functools.partial(middle_kernel, radius, tile, half, runs, names),
        grid_spec=pltpu.PrefetchScalarGridSpec(
            num_scalar_prefetch=1,
            grid=(1,),
            in_specs=[in_vmem()] * (4 + half + len(runs))
            + [anywhere()] * 4,
            out_specs=in_vmem(),
            scratch_shapes=[
                pltpu.VMEM((cols // LANES * mid, 2 * LANES), BF16),
                pltpu.VMEM((slots * mid, cols), BF16),
                pltpu.VMEM((slots * mid, cols), BF16),
                pltpu.VMEM((tile, cols), F32),
                pltpu.VMEM((2,) + inside.shape, F32),
                pltpu.SemaphoreType.DMA((4,)),
            ],
        ),
        out_shape=jax.ShapeDtypeStruct((tile, cols), F32),
        compiler_params=params(),
        cost_estimate=light(),
        name="middle",
    )(scal, *from_vmem([*bands, rim, *mine, *sib]), *mains, across, inside)


def update(radius, slots, names, info, lengths, total, est, inside, across):
    tile = est.shape[0]
    return pl.pallas_call(
        functools.partial(update_kernel, radius, tile, slots, names),
        grid_spec=pltpu.PrefetchScalarGridSpec(
            num_scalar_prefetch=2,
            grid=(1,),
            in_specs=[in_vmem()] * 4,
            out_specs=whole_spec(est.shape),
        ),
        out_shape=jax.ShapeDtypeStruct(est.shape, F32),
        compiler_params=params(),
        cost_estimate=light(),
        name="update",
    )(info, lengths, *from_vmem([total, est, across, inside]))


def per_device(estimate, views, psf, offsets, lengths):
    size = lax.axis_size("view")
    joined = lax.axis_size("joined")
    position = lax.axis_index("view")
    members = size // BLOCKS
    half = members // 2
    member, block = position // BLOCKS, position % BLOCKS
    planes, tile, cols = views.shape[1:]
    radius = (psf.shape[2] - 1) // 2
    margin = radius + MAXD
    stack = views[0]
    est = estimate[0]
    total_blocks = cols // LANES

    odd = lax.axis_index("joined") % 2
    twin = [(i, i ^ 1) for i in range(joined)]
    other = [(i, (i - 1 if i % 2 == 0 else i + 1) % joined) for i in range(joined)]

    def target(p, s):
        k, b = p // BLOCKS, p % BLOCKS
        t = (k % half + s + (1 if k // half == b else 0)) % half
        return 2 * (b * half + t) + k // half

    first = total_blocks * 8 // 16
    cut = ((0, first), (first, total_blocks))
    away = [
        2 * ((member % half + s + (member // half == block).astype(jnp.int32)) % half)
        for s in range(half)
    ]
    inner = (member // half == block).astype(jnp.int32)
    edge_at = (1 - odd) * (tile - margin)
    away = away + [1 - position % 2, inner, edge_at, tile - margin - edge_at]
    pair, core = position // 2, position % 2
    extra = {
        "odd": odd, "core": core, "block": pair // half, "place": pair % half,
        "row": position % planes,
    }
    names = {name: len(away) + i for i, name in enumerate(extra)}
    away = jnp.stack(away + list(extra.values())).astype(jnp.int32)
    starts = (2,) * half + (1,)
    top, bottom = slice(0, margin), slice(tile - margin, tile)
    low, high = slice(0, margin), slice(margin, 2 * margin)
    every = slice(None)

    def edge_pieces(c0, c1):
        at = slice(c0 * LANES, c1 * LANES)
        pieces = []
        for s in range(half):
            pieces.append((0, s, s, (every, top, at), (every, low)))
            pieces.append((0, s, s, (every, bottom, at), (every, high)))
        return pieces

    def view_send(parts):
        sent = []
        for s, x in enumerate(parts):
            pairs = [(p, target(p, s)) for p in range(size)]
            sent.append(lax.ppermute(x, "view", [(p, q) for p, q in pairs if p != q]))
        return sent

    def pair_send(runs, kept, own, after):
        others, mine = part_pair(away, runs, kept, own, after)
        return mine, [lax.ppermute(x, "view", [(p, p ^ 1) for p in range(size)]) for x in others]

    def edge_shape(c0, c1):
        return (2, 2 * margin, (c1 - c0) * LANES)

    packed_a = pack(
        away, starts, [stack], [], [edge_shape(*cut[0])] * half, edge_pieces(*cut[0]), "pack_first"
    )
    slab = pack(
        away, starts, [est], packed_a[:1], [(margin, cols)] * 2,
        [
            (0, 0, half + 2, (every,), (every,)),
            (0, 1, half + 3, (every,), (every,)),
        ],
        "pack_slab",
    )
    across = lax.ppermute(slab[1], "joined", other)
    inside = lax.ppermute(slab[0], "joined", twin)
    kept_a = view_send(packed_a)
    center = slice(margin, tile - margin)
    packed = pack(
        away, starts, [stack], slab[:1],
        [edge_shape(*cut[1])] * half + [(2, tile - 2 * margin, cols)] * half,
        edge_pieces(*cut[1])
        + [(0, half + s, s, (every, center), (every,)) for s in range(half)],
        "pack_second",
    )
    rim_middle, fx, fy, fy_low, by, by_low, bx, bm = prepare(
        radius, names, away, offsets, lengths, psf, est
    )
    packed_b, packed_c = list(packed[:half]), packed[half:]
    fellow = [(p, p ^ 1) for p in range(size)]
    runs_a, runs_b = [
        runs_of(arrays, half, c1 - c0) for arrays, (c0, c1) in zip((2, 1), cut)
    ]
    others, mine_a = part_pair(away, runs_a, kept_a, packed_a[-1], [rim_middle])
    others = list(others)
    others[0], others[1], across, inside = lax.optimization_barrier((others[0], others[1], across, inside))
    sib_a = [lax.ppermute(x, "view", fellow) for x in others]
    kept_b = view_send(packed_b)
    kept_c = view_send(packed_c)
    rims = forward(radius, cut, names, away, lengths, est, across, inside, fx, fy, fy_low)
    main, across, inside, *carries = edges(
        radius, tile, True, False, runs_a, names, away, (by, by_low, bx), rims[0], mine_a, sib_a, []
    )
    across = lax.ppermute(across, "joined", other)
    inside = lax.ppermute(inside, "joined", twin)
    chunks = [(main, inside, across)]
    mine, sib = pair_send(runs_b, kept_b, packed_b[-1], [main])
    main, across, inside = edges(
        radius, tile, False, True, runs_b, names, away, (by, by_low, bx), rims[1], mine, sib, carries
    )
    across = lax.ppermute(across, "joined", other)
    inside = lax.ppermute(inside, "joined", twin)
    chunks.append((main, inside, across))
    runs = runs_of(3, half, total_blocks)
    mine, sib = pair_send(runs, kept_c, packed_c[-1], [main, chunks[0][2], chunks[0][1]])
    mains = [chunk[0] for chunk in chunks]
    bands = (by, by_low, bm)
    total = middle(radius, tile, runs, names, away, bands, rim_middle, mine, sib, mains, *chunks[0][1:])
    out = update(radius, members, names, away, lengths, total, est, *chunks[1][1:])
    return out[None]


def solution(mesh):
    return jax.shard_map(
        per_device,
        mesh=mesh,
        in_specs=(P("view", "joined", None), P("view", None, "joined", None), P(), P(), P()),
        out_specs=P("view", "joined", None),
        check_vma=False,
    )
```

```python
import functools

import jax
import jax.numpy as jnp
from jax import lax
from jax.experimental import pallas as pl
from jax.experimental.pallas import tpu as pltpu
from jax.sharding import PartitionSpec as P

MAXD = 16
BLOCKS = 2
LANES = 128
F32 = jnp.float32
BF16 = jnp.bfloat16
VMEM_LIMIT = 28 * 1024 * 1024


def split(x):
    hi = x.astype(BF16)
    return hi, (x - hi.astype(F32)).astype(BF16)


def mm(a, b):
    return jnp.dot(a, b, preferred_element_type=F32)


def slot_view(info, names, slot, half):
    core, block = info[names["core"]], info[names["block"]]
    other = slot >= half
    if isinstance(slot, int):
        side = 1 - core if other else core
        turn = slot % half
    else:
        side = jnp.where(other, 1 - core, core)
        turn = lax.rem(slot, half)
    step = jnp.where(side == block, 1, 0)
    return side * half + lax.rem(info[names["place"]] - turn - step + 2 * half, half)


def alive(info, names, lengths, slot, half):
    view = slot_view(info, names, slot, half)
    return jnp.where(info[names["row"]] < lengths[info[names["block"]], view], 1.0, 0.0)


def toeplitz(row, rows, shift, width):
    turned = pltpu.roll(jnp.broadcast_to(row, (8, width)), lax.rem(shift + 4 * width, width), 1)
    wide = jnp.broadcast_to(turned[0:1], (rows, width))
    return pltpu.roll(wide, 0, 1, stride=1, stride_axis=0)


def side_by_side(left, right):
    hi, lo = split(jnp.concatenate([left, right], axis=1))
    return jnp.concatenate([hi, hi], axis=0), lo


def fetch(source, target, sem):
    copy = pltpu.make_async_copy(source, target, sem)
    copy.start()
    return copy


def fetch_sides(odd, inside, across, target, first_sem, second_sem):
    return [
        fetch(inside, target.at[1 - odd], first_sem),
        fetch(across, target.at[odd], second_sem),
    ]


def images(lhs, first, second, rows, blocks):
    part = mm(lhs[...], first) + mm(lhs[:, :LANES], second)
    result = []
    for j in range(blocks):
        n = (j + 1) % blocks
        here = part[j * rows : (j + 1) * rows, :LANES]
        result.append(here + part[n * rows : (n + 1) * rows, LANES:])
    return result


def spread(value, lhs):
    rows, cols = value.shape
    hi, lo = split(value)
    for j in range(cols // LANES):
        at = slice(j * LANES, (j + 1) * LANES)
        lhs[j * rows : (j + 1) * rows, :LANES] = hi[:, at]
        lhs[j * rows : (j + 1) * rows, LANES:] = lo[:, at]


def prepare_kernel(radius, names, info, offsets, lengths, psf, est, *refs):
    rim, fx, fy, fy_low, by, by_low, bx, bm, hi, lo, lhs, taps = refs
    slot = pl.program_id(0)
    half = rim.shape[0] // 2
    margin = radius + MAXD
    tile, cols = est.shape
    extended = tile + 2 * margin
    mid = tile - 2 * margin
    width = taps.shape[1]

    @pl.when(slot == 0)
    def _():
        hi[...], lo[...] = split(pltpu.roll(est[...], margin, 1))
        taps[...] = jnp.zeros(taps.shape, F32)

    view = slot_view(info, names, slot, half)
    dx, dy = offsets[0, view], offsets[1, view]
    weights = psf[view]
    taps[0:2, : 2 * radius + 1] = weights / jnp.sum(weights, axis=1, keepdims=True)
    gx, gy = taps[0:1, :], taps[1:2, :]
    band = toeplitz(gx, tile, dx + MAXD, width)
    back = jnp.transpose(band)[:extended, :]
    band = band[:, :extended]
    edge = jnp.concatenate([band[:margin], band[tile - margin :]], axis=0)
    fx[0] = jnp.concatenate(split(edge), axis=0)
    ahead = jnp.transpose(toeplitz(gy, LANES, dy + MAXD, width))
    fy[0], fy_low[0] = side_by_side(ahead[:LANES], ahead[LANES:])
    by[0], by_low[0] = side_by_side(
        toeplitz(gy, LANES, dy + MAXD - LANES, width)[:, :LANES],
        toeplitz(gy, LANES, dy + MAXD, width)[:, :LANES],
    )
    bx[...] = jnp.concatenate(split(back), axis=0)
    line = back[margin : margin + tile]
    wide = bm.shape[2]
    if wide > tile:
        line = jnp.concatenate([line, jnp.zeros((tile, wide - tile), F32)], axis=1)
    line = pltpu.roll(line, lax.rem(mid * slot - margin + wide, wide), 1)
    lane = lax.broadcasted_iota(jnp.int32, line.shape, 1)
    line = jnp.where((lane >= mid * slot) & (lane < mid * (slot + 1)), line, 0.0)
    bm[0] = jnp.concatenate(split(line), axis=0)

    b_hi, b_lo = split(band[margin : tile - margin, margin : margin + tile])
    both = mm(jnp.concatenate([b_hi, b_lo], axis=0), hi[...])
    spread(both[:mid] + both[mid:] + mm(b_hi, lo[...]), lhs)
    live = alive(info, names, lengths, slot, half)
    for j, image in enumerate(images(lhs, fy[0], fy_low[0], mid, cols // LANES)):
        rim[slot, :, j * LANES : (j + 1) * LANES] = live / image


def forward_kernel(radius, cut, names, info, lengths, est, across, inside, fx, fy, fy_low, *rest):
    outs, (e_hi, e_lo, lhs) = rest[:-3], rest[-3:]
    slot = pl.program_id(0)
    margin = radius + MAXD
    tile, cols = est.shape
    edge = 2 * margin
    even = info[names["odd"]] == 0

    def put(piece, at):
        rows = slice(at, at + piece.shape[0])
        e_hi[rows, :], e_lo[rows, :] = split(pltpu.roll(piece[...], margin, 1))

    @pl.when(slot == 0)
    def _():
        put(est, margin)

    @pl.when((slot == 0) & even)
    def _():
        put(across, 0)
        put(inside, margin + tile)

    @pl.when((slot == 0) & jnp.logical_not(even))
    def _():
        put(inside, 0)
        put(across, margin + tile)

    live = alive(info, names, lengths, slot, outs[0].shape[0] // 2)
    both = mm(fx[0], e_hi[...])
    spread(both[:edge] + both[edge:] + mm(fx[0, :edge], e_lo[...]), lhs)
    for j, image in enumerate(images(lhs, fy[0], fy_low[0], edge, cols // LANES)):
        for out, (c0, c1) in zip(outs, cut):
            if c0 <= j < c1:
                out[slot, :, (j - c0) * LANES : (j - c0 + 1) * LANES] = live / image


def ratio_blurred(value, lhs, first, second):
    rows, cols = value.shape
    spread(value, lhs)
    part = mm(lhs[...], first) + mm(lhs[:, :LANES], second)
    return [part[j * rows : (j + 1) * rows] for j in range(cols // LANES)]


def runs_of(arrays, half, blocks):
    total = half * blocks
    marks = [round(total * i / arrays) for i in range(arrays + 1)]
    result = []
    for lo, hi in zip(marks, marks[1:]):
        runs = []
        for view in range(half):
            c0, c1 = max(lo, view * blocks), min(hi, (view + 1) * blocks)
            if c0 < c1:
                runs.append((view, c0 - view * blocks, c1 - view * blocks))
        result.append(runs)
    return result


def slot_values(slot, half, runs, mine, sib):
    if slot < half:
        return mine[slot][...]
    parts = []
    for ref, of_ref in zip(sib, runs):
        at = 0
        for view, c0, c1 in of_ref:
            width = (c1 - c0) * LANES
            if view == slot - half:
                parts.append(ref[:, at : at + width])
            at += width
    return parts[0] if len(parts) == 1 else jnp.concatenate(parts, axis=1)


def pair_kernel(half, runs, scal, *refs):
    kept, own, refs = refs[:half], refs[half], refs[half + 1 :]
    outs, (buffer, sem) = refs[-2 - len(runs) - half : -2], refs[-2:]
    away, inner = scal[half], scal[half + 1]
    last = half - 1

    def part(view, source):
        for out, of_out in zip(outs, runs):
            at = 0
            for which, c0, c1 in of_out:
                width = (c1 - c0) * LANES
                if which == view:
                    out[:, at : at + width] = source[away, :, c0 * LANES : c1 * LANES]
                at += width
        outs[len(runs) + view][...] = source[1 - away]

    @pl.when(inner != 0)
    def _():
        copy = fetch(own, buffer, sem.at[0])
        for view in range(last):
            part(view, kept[view])
        copy.wait()
        part(last, buffer)

    @pl.when(inner == 0)
    def _():
        for view in range(half):
            part(view, kept[view])


def edge_kernel(radius, tile, is_first, is_last, half, runs, names, scal, by, by_low, bx, rim, *rest):
    mine, rest = rest[:half], rest[half:]
    sib, rest = rest[: len(runs)], rest[len(runs) :]
    carries = []
    if not is_first:
        carries, rest = rest[: 1 + is_last], rest[1 + is_last :]
    main, across, inside = rest[:3]
    rest = rest[3:]
    if not is_last:
        (next_left, *rest) = rest
    if is_first and not is_last:
        (next_right, *rest) = rest
    lhs, s_hi, s_lo = rest
    slots = 2 * half
    margin = radius + MAXD
    extended = tile + 2 * margin
    for slot in range(slots):
        value = slot_values(slot, half, runs, mine, sib) * rim[slot]
        parts = ratio_blurred(value, lhs, by[slot], by_low[slot])
        lefts = [x[:, :LANES] for x in parts]
        rights = [x[:, LANES:] for x in parts]
        if not is_first:
            lefts = [carries[0][slot]] + lefts
        else:
            if is_last:
                closing = rights[0]
            else:
                next_right[slot] = rights[0]
            rights = rights[1:]
        if is_last:
            rights = rights + [closing if is_first else carries[1][slot]]
        else:
            next_left[slot] = lefts[-1]
            lefts = lefts[:-1]
        base = slot * tile
        for j, (left, right) in enumerate(zip(lefts, rights)):
            at = slice(j * LANES, (j + 1) * LANES)
            hi, lo = split(left + right)
            for ref, piece in ((s_hi, hi), (s_lo, lo)):
                ref[base : base + margin, at] = piece[:margin]
                ref[base + margin : base + tile - margin, at] = jnp.zeros((tile - 2 * margin, LANES), BF16)
                ref[base + tile - margin : base + tile, at] = piece[margin:]
    both = mm(bx[...], s_hi[...])
    total = both[:extended] + both[extended:] + mm(bx[:extended], s_lo[...])
    odd = scal[names["odd"]] != 0
    main[...] = total[margin : margin + tile]
    inside[...] = jnp.where(odd, total[:margin], total[margin + tile :])
    across[...] = jnp.where(odd, total[margin + tile :], total[:margin])


def middle_kernel(radius, tile, half, runs, names, scal, by, by_low, bm, rim, *rest):
    mine, rest = rest[:half], rest[half:]
    sib, rest = rest[: len(runs)], rest[len(runs) :]
    first, second, across, inside, total, lhs, s_hi, s_lo = rest
    slots = 2 * half
    margin = radius + MAXD
    mid = tile - 2 * margin
    cols = total.shape[1]
    blocks = cols // LANES
    band = bm[0]
    for slot in range(1, slots):
        band = band + bm[slot]
    for slot in range(slots):
        value = slot_values(slot, half, runs, mine, sib) * rim[slot]
        parts = ratio_blurred(value, lhs, by[slot], by_low[slot])
        base = slot * mid
        for j in range(1, blocks + 1):
            at = slice((j - 1) * LANES, j * LANES)
            hi, lo = split(parts[j - 1][:, :LANES] + parts[j % blocks][:, LANES:])
            s_hi[base : base + mid, at] = hi
            s_lo[base : base + mid, at] = lo
    both = mm(band, s_hi[...])
    total[...] = both[:tile] + both[tile:] + mm(band[:tile], s_lo[...])
    width = first.shape[1]
    total[:, :width] += first[...]
    total[:, width:] += second[...]
    even = scal[names["odd"]] == 0
    add_rows(total, even, across, margin, 0)
    add_rows(total, jnp.logical_not(even), inside, margin, 0)


def add_rows(total, first, rows, margin, start):
    tile = total.shape[0]
    at = slice(start, start + rows.shape[1])

    @pl.when(first)
    def _():
        total[:margin, at] += rows[...]

    @pl.when(jnp.logical_not(first))
    def _():
        total[tile - margin :, at] += rows[...]


def update_kernel(radius, tile, slots, names, scal, lengths, total, est, across, inside, out):
    margin = radius + MAXD
    count = alive(scal, names, lengths, 0, slots // 2)
    for slot in range(1, slots):
        count += alive(scal, names, lengths, slot, slots // 2)
    width, cols = inside.shape[1], est.shape[1]
    weight = 1.0 / jnp.full((1, cols), count, F32)
    even = scal[names["odd"]] == 0
    add_rows(total, even, across, margin, cols - width)
    add_rows(total, jnp.logical_not(even), inside, margin, cols - width)
    out[...] = est[...] * weight * pltpu.roll(total[...], LANES - margin, 1)


def light():
    return pl.CostEstimate(flops=0, bytes_accessed=1024, transcendentals=0)


def pack_kernel(starts, pieces, n_in, *refs):
    scal, refs = refs[0], refs[1:]
    ins, outs, sem = refs[:n_in], refs[n_in:-1], refs[-1]
    copies = []
    for i, (src, dst, start, src_at, dst_at) in enumerate(pieces):
        ref = ins[src]
        if start is not None and start < len(starts):
            ref = ref.at[pl.ds(scal[start], starts[start])]
        elif start is not None:
            ref = ref.at[pl.ds(pl.multiple_of(scal[start], 8), outs[dst].shape[0])]
        copies.append(fetch(ref.at[src_at], outs[dst].at[dst_at], sem.at[i]))
    for copy in copies:
        copy.wait()


def in_vmem():
    return pl.BlockSpec(memory_space=pltpu.VMEM)


def in_hbm():
    return pl.BlockSpec(memory_space=pltpu.HBM)


def anywhere():
    return pl.BlockSpec(memory_space=pl.ANY)


def from_vmem(operands):
    return [pltpu.with_memory_space_constraint(x, pltpu.VMEM) for x in operands]


def from_hbm(operands):
    return [pltpu.with_memory_space_constraint(x, pltpu.HBM) for x in operands]


def pack(scal, starts, ins, after, shapes, pieces, name):
    return pl.pallas_call(
        functools.partial(pack_kernel, starts, pieces, len(ins) + len(after)),
        grid_spec=pltpu.PrefetchScalarGridSpec(
            num_scalar_prefetch=1,
            grid=(1,),
            in_specs=[in_hbm()] * len(ins) + [anywhere()] * len(after),
            out_specs=[in_vmem()] * len(shapes),
            scratch_shapes=[pltpu.SemaphoreType.DMA((len(pieces),))],
        ),
        out_shape=[jax.ShapeDtypeStruct(s, F32) for s in shapes],
        compiler_params=params(),
        cost_estimate=light(),
        name=name,
    )(scal, *from_hbm(ins), *after)


def part_pair(scal, runs, kept, own, after):
    half = len(kept)
    rows = own.shape[1]
    shapes = [(rows, sum(c1 - c0 for _, c0, c1 in of) * LANES) for of in runs]
    shapes += [(rows, own.shape[2])] * half
    out = pl.pallas_call(
        functools.partial(pair_kernel, half, runs),
        grid_spec=pltpu.PrefetchScalarGridSpec(
            num_scalar_prefetch=1,
            grid=(1,),
            in_specs=[in_vmem()] * half + [in_hbm()] + [anywhere()] * len(after),
            out_specs=[in_vmem()] * len(shapes),
            scratch_shapes=[pltpu.VMEM(own.shape, F32), pltpu.SemaphoreType.DMA((1,))],
        ),
        out_shape=[jax.ShapeDtypeStruct(s, F32) for s in shapes],
        compiler_params=params(),
        cost_estimate=light(),
        name="pair",
    )(scal, *from_vmem(kept), *from_hbm([own]), *after)
    return out[: len(runs)], out[len(runs) :]


def whole_spec(shape):
    return pl.BlockSpec(shape, lambda i, *_: (0,) * len(shape))


def params():
    return pltpu.CompilerParams(vmem_limit_bytes=VMEM_LIMIT, dimension_semantics=("arbitrary",))


def prepare(radius, names, info, offsets, lengths, psf, est):
    slots = psf.shape[0]
    tile, cols = est.shape
    margin = radius + MAXD
    mid, extended = tile - 2 * margin, tile + 2 * margin
    bands = [
        (slots, 4 * margin, extended),
        (slots, 2 * LANES, 2 * LANES),
        (slots, LANES, 2 * LANES),
        (slots, 2 * LANES, 2 * LANES),
        (slots, LANES, 2 * LANES),
        (2 * extended, slots * tile),
        (slots, 2 * tile, slots * mid),
    ]
    specs = [pl.BlockSpec((1,) + s[1:], lambda i, *_: (i, 0, 0)) for s in bands]
    specs[5] = pl.BlockSpec((2 * extended, tile), lambda i, *_: (0, i))
    return pl.pallas_call(
        functools.partial(prepare_kernel, radius, names),
        grid_spec=pltpu.PrefetchScalarGridSpec(
            num_scalar_prefetch=3,
            grid=(slots,),
            in_specs=[whole_spec(psf.shape), in_vmem()],
            out_specs=[in_vmem()] + specs,
            scratch_shapes=[
                pltpu.VMEM((tile, cols), BF16),
                pltpu.VMEM((tile, cols), BF16),
                pltpu.VMEM((mid * cols // LANES, 2 * LANES), BF16),
                pltpu.VMEM((8, 2 * LANES), F32),
            ],
        ),
        out_shape=[jax.ShapeDtypeStruct((slots, mid, cols), F32)]
        + [jax.ShapeDtypeStruct(s, BF16) for s in bands],
        compiler_params=params(),
        cost_estimate=light(),
        name="prepare",
    )(info, offsets, lengths, psf, *from_vmem([est]))


def forward(radius, cut, names, info, lengths, est, across, inside, fx, fy, fy_low):
    slots = fx.shape[0]
    tile, cols = est.shape
    margin = radius + MAXD
    shapes = [(slots, 2 * margin, (c1 - c0) * LANES) for c0, c1 in cut]
    extended = tile + 2 * margin
    return pl.pallas_call(
        functools.partial(forward_kernel, radius, cut, names),
        grid_spec=pltpu.PrefetchScalarGridSpec(
            num_scalar_prefetch=2,
            grid=(slots,),
            in_specs=[in_vmem()] * 3
            + [pl.BlockSpec((1,) + x.shape[1:], lambda i, *_: (i, 0, 0)) for x in (fx, fy, fy_low)],
            out_specs=[in_vmem()] * len(shapes),
            scratch_shapes=[
                pltpu.VMEM((extended, cols), BF16),
                pltpu.VMEM((extended, cols), BF16),
                pltpu.VMEM((2 * margin * cols // LANES, 2 * LANES), BF16),
            ],
        ),
        out_shape=[jax.ShapeDtypeStruct(s, F32) for s in shapes],
        compiler_params=params(),
        cost_estimate=light(),
        name="forward",
    )(info, lengths, *from_vmem([est, across, inside]), fx, fy, fy_low)


def edges(radius, tile, is_first, is_last, runs, names, scal, bands, rim, mine, sib, carries):
    half = len(mine)
    slots = 2 * half
    margin = radius + MAXD
    blocks = rim.shape[2] // LANES
    made = (blocks - (1 if is_first else 0) + (1 if is_last else 0)) * LANES
    shapes = [(tile, made), (margin, made), (margin, made)]
    carried = (slots, 2 * margin, LANES)
    if not is_last:
        shapes.append(carried)
        if is_first:
            shapes.append(carried)
    return pl.pallas_call(
        functools.partial(edge_kernel, radius, tile, is_first, is_last, half, runs, names),
        grid_spec=pltpu.PrefetchScalarGridSpec(
            num_scalar_prefetch=1,
            grid=(1,),
            in_specs=[in_vmem()] * (4 + half + len(sib) + len(carries)),
            out_specs=[in_vmem()] * len(shapes),
            scratch_shapes=[
                pltpu.VMEM((blocks * 2 * margin, 2 * LANES), BF16),
                pltpu.VMEM((slots * tile, made), BF16),
                pltpu.VMEM((slots * tile, made), BF16),
            ],
        ),
        out_shape=[jax.ShapeDtypeStruct(s, F32) for s in shapes],
        compiler_params=params(),
        cost_estimate=light(),
        name="edges",
    )(scal, *from_vmem([*bands, rim, *mine, *sib, *carries]))


def middle(radius, tile, runs, names, scal, bands, rim, mine, sib, mains, inside, across):
    half = len(mine)
    slots, mid, cols = rim.shape
    margin = radius + MAXD
    return pl.pallas_call(
        functools.partial(middle_kernel, radius, tile, half, runs, names),
        grid_spec=pltpu.PrefetchScalarGridSpec(
            num_scalar_prefetch=1,
            grid=(1,),
            in_specs=[in_vmem()] * (8 + half + len(runs)),
            out_specs=in_vmem(),
            scratch_shapes=[
                pltpu.VMEM((cols // LANES * mid, 2 * LANES), BF16),
                pltpu.VMEM((slots * mid, cols), BF16),
                pltpu.VMEM((slots * mid, cols), BF16),
            ],
        ),
        out_shape=jax.ShapeDtypeStruct((tile, cols), F32),
        compiler_params=params(),
        cost_estimate=light(),
        name="middle",
    )(scal, *from_vmem([*bands, rim, *mine, *sib, *mains, across, inside]))


def update(radius, slots, names, info, lengths, total, est, inside, across):
    tile = est.shape[0]
    return pl.pallas_call(
        functools.partial(update_kernel, radius, tile, slots, names),
        grid_spec=pltpu.PrefetchScalarGridSpec(
            num_scalar_prefetch=2,
            grid=(1,),
            in_specs=[in_vmem()] * 4,
            out_specs=whole_spec(est.shape),
        ),
        out_shape=jax.ShapeDtypeStruct(est.shape, F32),
        compiler_params=params(),
        cost_estimate=light(),
        name="update",
    )(info, lengths, *from_vmem([total, est, across, inside]))


def per_device(estimate, views, psf, offsets, lengths):
    size = lax.axis_size("view")
    joined = lax.axis_size("joined")
    position = lax.axis_index("view")
    members = size // BLOCKS
    half = members // 2
    member, block = position // BLOCKS, position % BLOCKS
    planes, tile, cols = views.shape[1:]
    radius = (psf.shape[2] - 1) // 2
    margin = radius + MAXD
    stack = views[0]
    est = estimate[0]
    total_blocks = cols // LANES

    odd = lax.axis_index("joined") % 2
    twin = [(i, i ^ 1) for i in range(joined)]
    other = [(i, (i - 1 if i % 2 == 0 else i + 1) % joined) for i in range(joined)]

    def target(p, s):
        k, b = p // BLOCKS, p % BLOCKS
        t = (k % half + s + (1 if k // half == b else 0)) % half
        return 2 * (b * half + t) + k // half

    first = total_blocks * 8 // 16
    cut = ((0, first), (first, total_blocks))
    away = [
        2 * ((member % half + s + (member // half == block).astype(jnp.int32)) % half)
        for s in range(half)
    ]
    inner = (member // half == block).astype(jnp.int32)
    edge_at = (1 - odd) * (tile - margin)
    away = away + [1 - position % 2, inner, edge_at, tile - margin - edge_at]
    pair, core = position // 2, position % 2
    extra = {
        "odd": odd, "core": core, "block": pair // half, "place": pair % half,
        "row": position % planes,
    }
    names = {name: len(away) + i for i, name in enumerate(extra)}
    away = jnp.stack(away + list(extra.values())).astype(jnp.int32)
    starts = (2,) * half + (1,)
    top, bottom = slice(0, margin), slice(tile - margin, tile)
    low, high = slice(0, margin), slice(margin, 2 * margin)
    every = slice(None)

    def edge_pieces(c0, c1):
        at = slice(c0 * LANES, c1 * LANES)
        pieces = []
        for s in range(half):
            pieces.append((0, s, s, (every, top, at), (every, low)))
            pieces.append((0, s, s, (every, bottom, at), (every, high)))
        return pieces

    def view_send(parts):
        sent = []
        for s, x in enumerate(parts):
            pairs = [(p, target(p, s)) for p in range(size)]
            sent.append(lax.ppermute(x, "view", [(p, q) for p, q in pairs if p != q]))
        return sent

    def pair_send(runs, kept, own, after):
        others, mine = part_pair(away, runs, kept, own, after)
        return mine, [lax.ppermute(x, "view", [(p, p ^ 1) for p in range(size)]) for x in others]

    def edge_shape(c0, c1):
        return (2, 2 * margin, (c1 - c0) * LANES)

    packed_a = pack(
        away, starts, [stack], [], [edge_shape(*cut[0])] * half, edge_pieces(*cut[0]), "pack_first"
    )
    slab = pack(
        away, starts, [est], packed_a[:1], [(margin, cols)] * 2,
        [
            (0, 0, half + 2, (every,), (every,)),
            (0, 1, half + 3, (every,), (every,)),
        ],
        "pack_slab",
    )
    across = lax.ppermute(slab[1], "joined", other)
    inside = lax.ppermute(slab[0], "joined", twin)
    kept_a = view_send(packed_a)
    center = slice(margin, tile - margin)
    packed = pack(
        away, starts, [stack], slab[:1],
        [edge_shape(*cut[1])] * half + [(2, tile - 2 * margin, cols)] * half,
        edge_pieces(*cut[1])
        + [(0, half + s, s, (every, center), (every,)) for s in range(half)],
        "pack_second",
    )
    rim_middle, fx, fy, fy_low, by, by_low, bx, bm = prepare(
        radius, names, away, offsets.T, lengths.T, psf, est
    )
    packed_b, packed_c = list(packed[:half]), packed[half:]
    fellow = [(p, p ^ 1) for p in range(size)]
    runs_a, runs_b = [
        runs_of(arrays, half, c1 - c0) for arrays, (c0, c1) in zip((2, 1), cut)
    ]
    others, mine_a = part_pair(away, runs_a, kept_a, packed_a[-1], [rim_middle])
    others = list(others)
    others[0], others[1], across, inside = lax.optimization_barrier((others[0], others[1], across, inside))
    sib_a = [lax.ppermute(x, "view", fellow) for x in others]
    kept_b = view_send(packed_b)
    kept_c = view_send(packed_c)
    rims = forward(radius, cut, names, away, lengths.T, est, across, inside, fx, fy, fy_low)
    main, across, inside, *carries = edges(
        radius, tile, True, False, runs_a, names, away, (by, by_low, bx), rims[0], mine_a, sib_a, []
    )
    across = lax.ppermute(across, "joined", other)
    inside = lax.ppermute(inside, "joined", twin)
    chunks = [(main, inside, across)]
    mine, sib = pair_send(runs_b, kept_b, packed_b[-1], [main])
    main, across, inside = edges(
        radius, tile, False, True, runs_b, names, away, (by, by_low, bx), rims[1], mine, sib, carries
    )
    across = lax.ppermute(across, "joined", other)
    inside = lax.ppermute(inside, "joined", twin)
    chunks.append((main, inside, across))
    runs = runs_of(3, half, total_blocks)
    mine, sib = pair_send(runs, kept_c, packed_c[-1], [main, chunks[0][2], chunks[0][1]])
    mains = [chunk[0] for chunk in chunks]
    bands = (by, by_low, bm)
    total = middle(radius, tile, runs, names, away, bands, rim_middle, mine, sib, mains, *chunks[0][1:])
    out = update(radius, members, names, away, lengths.T, total, est, *chunks[1][1:])
    return out[None]


def solution(mesh):
    return jax.shard_map(
        per_device,
        mesh=mesh,
        in_specs=(P("view", "joined", None), P("view", None, "joined", None), P(), P(), P()),
        out_specs=P("view", "joined", None),
        check_vma=False,
    )
```

```python
import functools

import jax
import jax.numpy as jnp
from jax import lax
from jax.experimental import pallas as pl
from jax.experimental.pallas import tpu as pltpu
from jax.sharding import PartitionSpec as P

MAXD = 16
BLOCKS = 2
LANES = 128
F32 = jnp.float32
BF16 = jnp.bfloat16
VMEM_LIMIT = 28 * 1024 * 1024


def split(x):
    hi = x.astype(BF16)
    return hi, (x - hi.astype(F32)).astype(BF16)


def mm(a, b):
    return jnp.dot(a, b, preferred_element_type=F32)


def slot_view(info, names, slot, half):
    core, block = info[names["core"]], info[names["block"]]
    other = slot >= half
    if isinstance(slot, int):
        side = 1 - core if other else core
        turn = slot % half
    else:
        side = jnp.where(other, 1 - core, core)
        turn = lax.rem(slot, half)
    step = jnp.where(side == block, 1, 0)
    return side * half + lax.rem(info[names["place"]] - turn - step + 2 * half, half)


def alive(info, names, lengths, slot, half):
    view = slot_view(info, names, slot, half)
    return jnp.where(info[names["row"]] < lengths[info[names["block"]], view], 1.0, 0.0)


def toeplitz(row, rows, shift, width):
    turned = pltpu.roll(jnp.broadcast_to(row, (8, width)), lax.rem(shift + 4 * width, width), 1)
    wide = jnp.broadcast_to(turned[0:1], (rows, width))
    return pltpu.roll(wide, 0, 1, stride=1, stride_axis=0)


def side_by_side(left, right):
    hi, lo = split(jnp.concatenate([left, right], axis=1))
    return jnp.concatenate([hi, hi], axis=0), lo


def fetch(source, target, sem):
    copy = pltpu.make_async_copy(source, target, sem)
    copy.start()
    return copy


def images(lhs, first, second, rows, blocks):
    part = mm(lhs[...], first) + mm(lhs[:, :LANES], second)
    result = []
    for j in range(blocks):
        n = (j + 1) % blocks
        here = part[j * rows : (j + 1) * rows, :LANES]
        result.append(here + part[n * rows : (n + 1) * rows, LANES:])
    return result


def spread(value, lhs):
    rows, cols = value.shape
    hi, lo = split(value)
    for j in range(cols // LANES):
        at = slice(j * LANES, (j + 1) * LANES)
        lhs[j * rows : (j + 1) * rows, :LANES] = hi[:, at]
        lhs[j * rows : (j + 1) * rows, LANES:] = lo[:, at]


def prepare_kernel(radius, names, info, offsets, lengths, psf, est, *refs):
    rim, fx, fy, fy_low, by, by_low, bx, bm, hi, lo, lhs, taps = refs
    slot = pl.program_id(0)
    half = rim.shape[0] // 2
    margin = radius + MAXD
    tile, cols = est.shape
    extended = tile + 2 * margin
    mid = tile - 2 * margin
    width = taps.shape[1]

    @pl.when(slot == 0)
    def _():
        hi[...], lo[...] = split(pltpu.roll(est[...], margin, 1))
        taps[...] = jnp.zeros(taps.shape, F32)

    view = slot_view(info, names, slot, half)
    dx, dy = offsets[0, view], offsets[1, view]
    weights = psf[view]
    taps[0:2, : 2 * radius + 1] = weights / jnp.sum(weights, axis=1, keepdims=True)
    gx, gy = taps[0:1, :], taps[1:2, :]
    band = toeplitz(gx, tile, dx + MAXD, width)
    back = jnp.transpose(band)[:extended, :]
    band = band[:, :extended]
    edge = jnp.concatenate([band[:margin], band[tile - margin :]], axis=0)
    fx[0] = jnp.concatenate(split(edge), axis=0)
    ahead = jnp.transpose(toeplitz(gy, LANES, dy + MAXD, width))
    fy[0], fy_low[0] = side_by_side(ahead[:LANES], ahead[LANES:])
    by[0], by_low[0] = side_by_side(
        toeplitz(gy, LANES, dy + MAXD - LANES, width)[:, :LANES],
        toeplitz(gy, LANES, dy + MAXD, width)[:, :LANES],
    )
    bx[...] = jnp.concatenate(split(back), axis=0)
    line = back[margin : margin + tile]
    wide = bm.shape[2]
    if wide > tile:
        line = jnp.concatenate([line, jnp.zeros((tile, wide - tile), F32)], axis=1)
    line = pltpu.roll(line, lax.rem(mid * slot - margin + wide, wide), 1)
    lane = lax.broadcasted_iota(jnp.int32, line.shape, 1)
    line = jnp.where((lane >= mid * slot) & (lane < mid * (slot + 1)), line, 0.0)
    bm[0] = jnp.concatenate(split(line), axis=0)

    b_hi, b_lo = split(band[margin : tile - margin, margin : margin + tile])
    both = mm(jnp.concatenate([b_hi, b_lo], axis=0), hi[...])
    spread(both[:mid] + both[mid:] + mm(b_hi, lo[...]), lhs)
    live = alive(info, names, lengths, slot, half)
    for j, image in enumerate(images(lhs, fy[0], fy_low[0], mid, cols // LANES)):
        rim[slot, :, j * LANES : (j + 1) * LANES] = live / image


def forward_kernel(radius, cut, names, info, lengths, est, across, inside, fx, fy, fy_low, *rest):
    outs, (e_hi, e_lo, lhs) = rest[:-3], rest[-3:]
    slot = pl.program_id(0)
    margin = radius + MAXD
    tile, cols = est.shape
    edge = 2 * margin
    even = info[names["odd"]] == 0

    def put(piece, at):
        rows = slice(at, at + piece.shape[0])
        e_hi[rows, :], e_lo[rows, :] = split(pltpu.roll(piece[...], margin, 1))

    @pl.when(slot == 0)
    def _():
        put(est, margin)

    @pl.when((slot == 0) & even)
    def _():
        put(across, 0)
        put(inside, margin + tile)

    @pl.when((slot == 0) & jnp.logical_not(even))
    def _():
        put(inside, 0)
        put(across, margin + tile)

    live = alive(info, names, lengths, slot, outs[0].shape[0] // 2)
    both = mm(fx[0], e_hi[...])
    spread(both[:edge] + both[edge:] + mm(fx[0, :edge], e_lo[...]), lhs)
    for j, image in enumerate(images(lhs, fy[0], fy_low[0], edge, cols // LANES)):
        for out, (c0, c1) in zip(outs, cut):
            if c0 <= j < c1:
                out[slot, :, (j - c0) * LANES : (j - c0 + 1) * LANES] = live / image


def ratio_blurred(value, lhs, first, second):
    rows, cols = value.shape
    spread(value, lhs)
    part = mm(lhs[...], first) + mm(lhs[:, :LANES], second)
    return [part[j * rows : (j + 1) * rows] for j in range(cols // LANES)]


def runs_of(arrays, half, blocks):
    total = half * blocks
    marks = [round(total * i / arrays) for i in range(arrays + 1)]
    result = []
    for lo, hi in zip(marks, marks[1:]):
        runs = []
        for view in range(half):
            c0, c1 = max(lo, view * blocks), min(hi, (view + 1) * blocks)
            if c0 < c1:
                runs.append((view, c0 - view * blocks, c1 - view * blocks))
        result.append(runs)
    return result


def slot_values(slot, half, runs, mine, sib):
    if slot < half:
        return mine[slot][...]
    parts = []
    for ref, of_ref in zip(sib, runs):
        at = 0
        for view, c0, c1 in of_ref:
            width = (c1 - c0) * LANES
            if view == slot - half:
                parts.append(ref[:, at : at + width])
            at += width
    return parts[0] if len(parts) == 1 else jnp.concatenate(parts, axis=1)


def pair_kernel(half, runs, scal, *refs):
    kept, own, refs = refs[:half], refs[half], refs[half + 1 :]
    outs = refs[-len(runs) - half :]
    away, inner = scal[half], scal[half + 1]
    last = half - 1

    def part(view, source):
        for out, of_out in zip(outs, runs):
            at = 0
            for which, c0, c1 in of_out:
                width = (c1 - c0) * LANES
                if which == view:
                    out[:, at : at + width] = source[away, :, c0 * LANES : c1 * LANES]
                at += width
        outs[len(runs) + view][...] = source[1 - away]

    @pl.when(inner != 0)
    def _():
        for view in range(last):
            part(view, kept[view])
        part(last, own)

    @pl.when(inner == 0)
    def _():
        for view in range(half):
            part(view, kept[view])


def edge_kernel(radius, tile, is_first, is_last, half, runs, names, scal, by, by_low, bx, rim, *rest):
    mine, rest = rest[:half], rest[half:]
    sib, rest = rest[: len(runs)], rest[len(runs) :]
    carries = []
    if not is_first:
        carries, rest = rest[: 1 + is_last], rest[1 + is_last :]
    main, across, inside = rest[:3]
    rest = rest[3:]
    if not is_last:
        (next_left, *rest) = rest
    if is_first and not is_last:
        (next_right, *rest) = rest
    lhs, s_hi, s_lo = rest
    slots = 2 * half
    margin = radius + MAXD
    extended = tile + 2 * margin
    for slot in range(slots):
        value = slot_values(slot, half, runs, mine, sib) * rim[slot]
        parts = ratio_blurred(value, lhs, by[slot], by_low[slot])
        lefts = [x[:, :LANES] for x in parts]
        rights = [x[:, LANES:] for x in parts]
        if not is_first:
            lefts = [carries[0][slot]] + lefts
        else:
            if is_last:
                closing = rights[0]
            else:
                next_right[slot] = rights[0]
            rights = rights[1:]
        if is_last:
            rights = rights + [closing if is_first else carries[1][slot]]
        else:
            next_left[slot] = lefts[-1]
            lefts = lefts[:-1]
        base = slot * tile
        for j, (left, right) in enumerate(zip(lefts, rights)):
            at = slice(j * LANES, (j + 1) * LANES)
            hi, lo = split(left + right)
            for ref, piece in ((s_hi, hi), (s_lo, lo)):
                ref[base : base + margin, at] = piece[:margin]
                ref[base + margin : base + tile - margin, at] = jnp.zeros((tile - 2 * margin, LANES), BF16)
                ref[base + tile - margin : base + tile, at] = piece[margin:]
    both = mm(bx[...], s_hi[...])
    total = both[:extended] + both[extended:] + mm(bx[:extended], s_lo[...])
    odd = scal[names["odd"]] != 0
    main[...] = total[margin : margin + tile]
    inside[...] = jnp.where(odd, total[:margin], total[margin + tile :])
    across[...] = jnp.where(odd, total[margin + tile :], total[:margin])


def middle_kernel(radius, tile, half, runs, names, scal, by, by_low, bm, rim, *rest):
    mine, rest = rest[:half], rest[half:]
    sib, rest = rest[: len(runs)], rest[len(runs) :]
    first, second, across, inside, total, lhs, s_hi, s_lo = rest
    slots = 2 * half
    margin = radius + MAXD
    mid = tile - 2 * margin
    cols = total.shape[1]
    blocks = cols // LANES
    band = bm[0]
    for slot in range(1, slots):
        band = band + bm[slot]
    for slot in range(slots):
        value = slot_values(slot, half, runs, mine, sib) * rim[slot]
        parts = ratio_blurred(value, lhs, by[slot], by_low[slot])
        base = slot * mid
        for j in range(1, blocks + 1):
            at = slice((j - 1) * LANES, j * LANES)
            hi, lo = split(parts[j - 1][:, :LANES] + parts[j % blocks][:, LANES:])
            s_hi[base : base + mid, at] = hi
            s_lo[base : base + mid, at] = lo
    both = mm(band, s_hi[...])
    total[...] = both[:tile] + both[tile:] + mm(band[:tile], s_lo[...])
    width = first.shape[1]
    total[:, :width] += first[...]
    total[:, width:] += second[...]
    even = scal[names["odd"]] == 0
    add_rows(total, even, across, margin, 0)
    add_rows(total, jnp.logical_not(even), inside, margin, 0)


def add_rows(total, first, rows, margin, start):
    tile = total.shape[0]
    at = slice(start, start + rows.shape[1])

    @pl.when(first)
    def _():
        total[:margin, at] += rows[...]

    @pl.when(jnp.logical_not(first))
    def _():
        total[tile - margin :, at] += rows[...]


def update_kernel(radius, tile, slots, names, scal, lengths, total, est, across, inside, out):
    margin = radius + MAXD
    count = alive(scal, names, lengths, 0, slots // 2)
    for slot in range(1, slots):
        count += alive(scal, names, lengths, slot, slots // 2)
    width, cols = inside.shape[1], est.shape[1]
    weight = 1.0 / jnp.full((1, cols), count, F32)
    even = scal[names["odd"]] == 0
    add_rows(total, even, across, margin, cols - width)
    add_rows(total, jnp.logical_not(even), inside, margin, cols - width)
    out[...] = est[...] * weight * pltpu.roll(total[...], LANES - margin, 1)


def light():
    return pl.CostEstimate(flops=0, bytes_accessed=1024, transcendentals=0)


def pack_kernel(starts, pieces, n_in, *refs):
    scal, refs = refs[0], refs[1:]
    ins, outs, sem = refs[:n_in], refs[n_in:-1], refs[-1]
    copies = []
    for i, (src, dst, start, src_at, dst_at) in enumerate(pieces):
        ref = ins[src]
        if start is not None and start < len(starts):
            ref = ref.at[pl.ds(scal[start], starts[start])]
        elif start is not None:
            ref = ref.at[pl.ds(pl.multiple_of(scal[start], 8), outs[dst].shape[0])]
        copies.append(fetch(ref.at[src_at], outs[dst].at[dst_at], sem.at[i]))
    for copy in copies:
        copy.wait()


def in_vmem():
    return pl.BlockSpec(memory_space=pltpu.VMEM)


def in_hbm():
    return pl.BlockSpec(memory_space=pltpu.HBM)


def anywhere():
    return pl.BlockSpec(memory_space=pl.ANY)


def from_vmem(operands):
    return [pltpu.with_memory_space_constraint(x, pltpu.VMEM) for x in operands]


def from_hbm(operands):
    return [pltpu.with_memory_space_constraint(x, pltpu.HBM) for x in operands]


def pack(scal, starts, ins, after, shapes, pieces, name):
    return pl.pallas_call(
        functools.partial(pack_kernel, starts, pieces, len(ins) + len(after)),
        grid_spec=pltpu.PrefetchScalarGridSpec(
            num_scalar_prefetch=1,
            grid=(1,),
            in_specs=[in_hbm()] * len(ins) + [anywhere()] * len(after),
            out_specs=[in_vmem()] * len(shapes),
            scratch_shapes=[pltpu.SemaphoreType.DMA((len(pieces),))],
        ),
        out_shape=[jax.ShapeDtypeStruct(s, F32) for s in shapes],
        compiler_params=params(),
        cost_estimate=light(),
        name=name,
    )(scal, *from_hbm(ins), *after)


def part_pair(scal, runs, kept, own, after):
    half = len(kept)
    rows = own.shape[1]
    shapes = [(rows, sum(c1 - c0 for _, c0, c1 in of) * LANES) for of in runs]
    shapes += [(rows, own.shape[2])] * half
    out = pl.pallas_call(
        functools.partial(pair_kernel, half, runs),
        grid_spec=pltpu.PrefetchScalarGridSpec(
            num_scalar_prefetch=1,
            grid=(1,),
            in_specs=[in_vmem()] * (half + 1) + [anywhere()] * len(after),
            out_specs=[in_vmem()] * len(shapes),
        ),
        out_shape=[jax.ShapeDtypeStruct(s, F32) for s in shapes],
        compiler_params=params(),
        cost_estimate=light(),
        name="pair",
    )(scal, *from_vmem([*kept, own]), *after)
    return out[: len(runs)], out[len(runs) :]


def whole_spec(shape):
    return pl.BlockSpec(shape, lambda i, *_: (0,) * len(shape))


def params():
    return pltpu.CompilerParams(vmem_limit_bytes=VMEM_LIMIT, dimension_semantics=("arbitrary",))


def prepare(radius, names, info, offsets, lengths, psf, est):
    slots = psf.shape[0]
    tile, cols = est.shape
    margin = radius + MAXD
    mid, extended = tile - 2 * margin, tile + 2 * margin
    bands = [
        (slots, 4 * margin, extended),
        (slots, 2 * LANES, 2 * LANES),
        (slots, LANES, 2 * LANES),
        (slots, 2 * LANES, 2 * LANES),
        (slots, LANES, 2 * LANES),
        (2 * extended, slots * tile),
        (slots, 2 * tile, slots * mid),
    ]
    specs = [pl.BlockSpec((1,) + s[1:], lambda i, *_: (i, 0, 0)) for s in bands]
    specs[5] = pl.BlockSpec((2 * extended, tile), lambda i, *_: (0, i))
    return pl.pallas_call(
        functools.partial(prepare_kernel, radius, names),
        grid_spec=pltpu.PrefetchScalarGridSpec(
            num_scalar_prefetch=3,
            grid=(slots,),
            in_specs=[whole_spec(psf.shape), in_vmem()],
            out_specs=[in_vmem()] + specs,
            scratch_shapes=[
                pltpu.VMEM((tile, cols), BF16),
                pltpu.VMEM((tile, cols), BF16),
                pltpu.VMEM((mid * cols // LANES, 2 * LANES), BF16),
                pltpu.VMEM((8, 2 * LANES), F32),
            ],
        ),
        out_shape=[jax.ShapeDtypeStruct((slots, mid, cols), F32)]
        + [jax.ShapeDtypeStruct(s, BF16) for s in bands],
        compiler_params=params(),
        cost_estimate=light(),
        name="prepare",
    )(info, offsets, lengths, psf, *from_vmem([est]))


def forward(radius, cut, names, info, lengths, est, across, inside, fx, fy, fy_low):
    slots = fx.shape[0]
    tile, cols = est.shape
    margin = radius + MAXD
    shapes = [(slots, 2 * margin, (c1 - c0) * LANES) for c0, c1 in cut]
    extended = tile + 2 * margin
    return pl.pallas_call(
        functools.partial(forward_kernel, radius, cut, names),
        grid_spec=pltpu.PrefetchScalarGridSpec(
            num_scalar_prefetch=2,
            grid=(slots,),
            in_specs=[in_vmem()] * 3
            + [pl.BlockSpec((1,) + x.shape[1:], lambda i, *_: (i, 0, 0)) for x in (fx, fy, fy_low)],
            out_specs=[in_vmem()] * len(shapes),
            scratch_shapes=[
                pltpu.VMEM((extended, cols), BF16),
                pltpu.VMEM((extended, cols), BF16),
                pltpu.VMEM((2 * margin * cols // LANES, 2 * LANES), BF16),
            ],
        ),
        out_shape=[jax.ShapeDtypeStruct(s, F32) for s in shapes],
        compiler_params=params(),
        cost_estimate=light(),
        name="forward",
    )(info, lengths, *from_vmem([est, across, inside]), fx, fy, fy_low)


def edges(radius, tile, is_first, is_last, runs, names, scal, bands, rim, mine, sib, carries):
    half = len(mine)
    slots = 2 * half
    margin = radius + MAXD
    blocks = rim.shape[2] // LANES
    made = (blocks - (1 if is_first else 0) + (1 if is_last else 0)) * LANES
    shapes = [(tile, made), (margin, made), (margin, made)]
    carried = (slots, 2 * margin, LANES)
    if not is_last:
        shapes.append(carried)
        if is_first:
            shapes.append(carried)
    return pl.pallas_call(
        functools.partial(edge_kernel, radius, tile, is_first, is_last, half, runs, names),
        grid_spec=pltpu.PrefetchScalarGridSpec(
            num_scalar_prefetch=1,
            grid=(1,),
            in_specs=[in_vmem()] * (4 + half + len(sib) + len(carries)),
            out_specs=[in_vmem()] * len(shapes),
            scratch_shapes=[
                pltpu.VMEM((blocks * 2 * margin, 2 * LANES), BF16),
                pltpu.VMEM((slots * tile, made), BF16),
                pltpu.VMEM((slots * tile, made), BF16),
            ],
        ),
        out_shape=[jax.ShapeDtypeStruct(s, F32) for s in shapes],
        compiler_params=params(),
        cost_estimate=light(),
        name="edges",
    )(scal, *from_vmem([*bands, rim, *mine, *sib, *carries]))


def middle(radius, tile, runs, names, scal, bands, rim, mine, sib, mains, inside, across):
    half = len(mine)
    slots, mid, cols = rim.shape
    margin = radius + MAXD
    return pl.pallas_call(
        functools.partial(middle_kernel, radius, tile, half, runs, names),
        grid_spec=pltpu.PrefetchScalarGridSpec(
            num_scalar_prefetch=1,
            grid=(1,),
            in_specs=[in_vmem()] * (8 + half + len(runs)),
            out_specs=in_vmem(),
            scratch_shapes=[
                pltpu.VMEM((cols // LANES * mid, 2 * LANES), BF16),
                pltpu.VMEM((slots * mid, cols), BF16),
                pltpu.VMEM((slots * mid, cols), BF16),
            ],
        ),
        out_shape=jax.ShapeDtypeStruct((tile, cols), F32),
        compiler_params=params(),
        cost_estimate=light(),
        name="middle",
    )(scal, *from_vmem([*bands, rim, *mine, *sib, *mains, across, inside]))


def update(radius, slots, names, info, lengths, total, est, inside, across):
    tile = est.shape[0]
    return pl.pallas_call(
        functools.partial(update_kernel, radius, tile, slots, names),
        grid_spec=pltpu.PrefetchScalarGridSpec(
            num_scalar_prefetch=2,
            grid=(1,),
            in_specs=[in_vmem()] * 4,
            out_specs=whole_spec(est.shape),
        ),
        out_shape=jax.ShapeDtypeStruct(est.shape, F32),
        compiler_params=params(),
        cost_estimate=light(),
        name="update",
    )(info, lengths, *from_vmem([total, est, across, inside]))


def per_device(estimate, views, psf, offsets, lengths):
    size = lax.axis_size("view")
    joined = lax.axis_size("joined")
    position = lax.axis_index("view")
    members = size // BLOCKS
    half = members // 2
    member, block = position // BLOCKS, position % BLOCKS
    planes, tile, cols = views.shape[1:]
    radius = (psf.shape[2] - 1) // 2
    margin = radius + MAXD
    stack = views[0]
    est = estimate[0]
    total_blocks = cols // LANES

    odd = lax.axis_index("joined") % 2
    twin = [(i, i ^ 1) for i in range(joined)]
    other = [(i, (i - 1 if i % 2 == 0 else i + 1) % joined) for i in range(joined)]

    def target(p, s):
        k, b = p // BLOCKS, p % BLOCKS
        t = (k % half + s + (1 if k // half == b else 0)) % half
        return 2 * (b * half + t) + k // half

    first = total_blocks * 8 // 16
    cut = ((0, first), (first, total_blocks))
    away = [
        2 * ((member % half + s + (member // half == block).astype(jnp.int32)) % half)
        for s in range(half)
    ]
    inner = (member // half == block).astype(jnp.int32)
    edge_at = (1 - odd) * (tile - margin)
    away = away + [1 - position % 2, inner, edge_at, tile - margin - edge_at]
    pair, core = position // 2, position % 2
    extra = {
        "odd": odd, "core": core, "block": pair // half, "place": pair % half,
        "row": position % planes,
    }
    names = {name: len(away) + i for i, name in enumerate(extra)}
    away = jnp.stack(away + list(extra.values())).astype(jnp.int32)
    starts = (2,) * half + (1,)
    top, bottom = slice(0, margin), slice(tile - margin, tile)
    low, high = slice(0, margin), slice(margin, 2 * margin)
    every = slice(None)

    def edge_pieces(c0, c1):
        at = slice(c0 * LANES, c1 * LANES)
        pieces = []
        for s in range(half):
            pieces.append((0, s, s, (every, top, at), (every, low)))
            pieces.append((0, s, s, (every, bottom, at), (every, high)))
        return pieces

    def view_send(parts):
        sent = []
        for s, x in enumerate(parts):
            pairs = [(p, target(p, s)) for p in range(size)]
            sent.append(lax.ppermute(x, "view", [(p, q) for p, q in pairs if p != q]))
        return sent

    def pair_send(runs, kept, own, after):
        others, mine = part_pair(away, runs, kept, own, after)
        return mine, [lax.ppermute(x, "view", [(p, p ^ 1) for p in range(size)]) for x in others]

    def edge_shape(c0, c1):
        return (2, 2 * margin, (c1 - c0) * LANES)

    packed_a = pack(
        away, starts, [stack], [], [edge_shape(*cut[0])] * half, edge_pieces(*cut[0]), "pack_first"
    )
    slab = pack(
        away, starts, [est], packed_a[:1], [(margin, cols)] * 2,
        [
            (0, 0, half + 2, (every,), (every,)),
            (0, 1, half + 3, (every,), (every,)),
        ],
        "pack_slab",
    )
    across = lax.ppermute(slab[1], "joined", other)
    inside = lax.ppermute(slab[0], "joined", twin)
    kept_a = view_send(packed_a)
    center = slice(margin, tile - margin)
    packed = pack(
        away, starts, [stack], slab[:1],
        [edge_shape(*cut[1])] * half + [(2, tile - 2 * margin, cols)] * half,
        edge_pieces(*cut[1])
        + [(0, half + s, s, (every, center), (every,)) for s in range(half)],
        "pack_second",
    )
    rim_middle, fx, fy, fy_low, by, by_low, bx, bm = prepare(
        radius, names, away, offsets.T, lengths.T, psf, est
    )
    packed_b, packed_c = list(packed[:half]), packed[half:]
    fellow = [(p, p ^ 1) for p in range(size)]
    runs_a, runs_b = [
        runs_of(arrays, half, c1 - c0) for arrays, (c0, c1) in zip((2, 1), cut)
    ]
    others, mine_a = part_pair(away, runs_a, kept_a, packed_a[-1], [rim_middle])
    others = list(others)
    others[0], others[1], across, inside = lax.optimization_barrier((others[0], others[1], across, inside))
    sib_a = [lax.ppermute(x, "view", fellow) for x in others]
    kept_b = view_send(packed_b)
    kept_c = view_send(packed_c)
    rims = forward(radius, cut, names, away, lengths.T, est, across, inside, fx, fy, fy_low)
    main, across, inside, *carries = edges(
        radius, tile, True, False, runs_a, names, away, (by, by_low, bx), rims[0], mine_a, sib_a, []
    )
    across = lax.ppermute(across, "joined", other)
    inside = lax.ppermute(inside, "joined", twin)
    chunks = [(main, inside, across)]
    mine, sib = pair_send(runs_b, kept_b, packed_b[-1], [main])
    main, across, inside = edges(
        radius, tile, False, True, runs_b, names, away, (by, by_low, bx), rims[1], mine, sib, carries
    )
    across = lax.ppermute(across, "joined", other)
    inside = lax.ppermute(inside, "joined", twin)
    chunks.append((main, inside, across))
    runs = runs_of(3, half, total_blocks)
    mine, sib = pair_send(runs, kept_c, packed_c[-1], [main])
    mains = [chunk[0] for chunk in chunks]
    bands = (by, by_low, bm)
    total = middle(radius, tile, runs, names, away, bands, rim_middle, mine, sib, mains, *chunks[0][1:])
    out = update(radius, members, names, away, lengths.T, total, est, *chunks[1][1:])
    return out[None]


def solution(mesh):
    return jax.shard_map(
        per_device,
        mesh=mesh,
        in_specs=(P("view", "joined", None), P("view", None, "joined", None), P(), P(), P()),
        out_specs=P("view", "joined", None),
        check_vma=False,
    )
```
